128 devices in a mesh: member: 8 (over y, z_hi), domain: 16 (over z_lo, x, core).
Axes of the slice: x: 4, y: 4, z: 4 (z_hi: 2, z_lo: 2; z = z_hi * 2 + z_lo), core: 2. Of those that a mesh axis runs over, the one named last changes fastest.
Arguments:
- ensemble: float32 [80, 4, 3, 16, 4096], P('member', None, None, None, 'domain'), may hold values from -9 to 9
- velocity: float32 [2, 3, 16, 4096], P(None, None, None, 'domain'), may hold values from -0.5 to 0.5
- diffusivity: float32 [4], replicated, may hold values from 0.05 to 0.2
- land_mask: int32 [16, 4096], P(None, 'domain'), may hold values from 0 to 1
- obs_index: int32 [4, 8, 4], replicated, may hold values from 0 to 255, as said below
- obs_owner: int32 [4], replicated, may hold values from 0 to 127, as said below
- obs_value: float32 [4, 8], replicated, may hold values from -4 to 4
- obs_error: float32 [4, 8], replicated, may hold values from 0.2 to 1
Outputs:
- analysis: float32 [80, 4, 3, 16, 4096], P(None, None, None, 'member', 'domain')
The draws below stay inside these ranges and needn't reach their ends.
Inputs may be any that keep to these rules, and one draw needn't show every extreme that they name: `obs_index`: each observed cell has land_mask 1. The first observation of batch 0 is field 0, level 0 at its block's first row and column; the last observation of batch 3 is field 3, level 2 at its block's last row and column. A device's number is its member index times the number of domain tiles plus its domain index. obs_owner[0] is the first device and obs_owner[3] the last.
All inputs are finite; a program needn't handle non-finite values.
Results may differ from the reference program's by a relative error of at most 0.0001.
Values sent between devices are 32-bit elements; how exact they have to be, the bound alone decides.
A program may use at most 192 MiB of HBM per device.

```python
import math
import jax
import jax.numpy as jnp
from jax import lax

MEMBERS = 80
FIELDS = 4
LEVELS = 3
ROWS = 16
COLS_DEV = 256
BATCHES = 4
OBS_BATCH = 8
LOC_RADIUS = 64
ROWS_DEV = 2
COLS = 4096
N_DOMAIN = 16


def observation_tables(key):
    keys = jax.random.split(jax.random.fold_in(key, 101), 5)
    domain_total = COLS // COLS_DEV
    device_total = domain_total * (ROWS // ROWS_DEV)
    owner_dev = jax.random.randint(keys[0], (BATCHES,), 0, device_total, dtype=jnp.int32)
    owner_dev = owner_dev.at[0].set(0).at[BATCHES - 1].set(device_total - 1)
    local_row = jax.random.randint(keys[1], (BATCHES, OBS_BATCH), 0, ROWS_DEV, dtype=jnp.int32)
    local_row = local_row.at[0, 0].set(0).at[BATCHES - 1, OBS_BATCH - 1].set(ROWS_DEV - 1)
    local_col = jax.random.randint(keys[2], (BATCHES, OBS_BATCH), 0, COLS_DEV, dtype=jnp.int32)
    local_col = local_col.at[0, 0].set(0).at[BATCHES - 1, OBS_BATCH - 1].set(COLS_DEV - 1)
    field_num = jax.random.randint(keys[3], (BATCHES, OBS_BATCH), 0, FIELDS, dtype=jnp.int32)
    field_num = field_num.at[0, 0].set(0).at[BATCHES - 1, OBS_BATCH - 1].set(FIELDS - 1)
    level_num = jax.random.randint(keys[4], (BATCHES, OBS_BATCH), 0, LEVELS, dtype=jnp.int32)
    level_num = level_num.at[0, 0].set(0).at[BATCHES - 1, OBS_BATCH - 1].set(LEVELS - 1)
    table = jnp.stack([field_num, level_num, local_row, local_col], axis=-1).astype(jnp.int32)
    grid_row = (owner_dev // domain_total)[:, None] * ROWS_DEV + local_row
    grid_col = (owner_dev % domain_total)[:, None] * COLS_DEV + local_col
    return (owner_dev, table, grid_row, grid_col)


def draw_obs_owner(key, part):
    owner_dev, table, grid_row, grid_col = observation_tables(key)
    return owner_dev


def draw_obs_index(key, part):
    owner_dev, table, grid_row, grid_col = observation_tables(key)
    return table


def draw_land_mask(key, part):
    owner_dev, table, grid_row, grid_col = observation_tables(key)
    levels_drawn = jax.random.randint(jax.random.fold_in(key, 202), (ROWS, COLS), 0, 5, dtype=jnp.int32)
    ocean = (levels_drawn > 0).astype(jnp.int32)
    return ocean.at[grid_row.reshape(-1), grid_col.reshape(-1)].set(1)


def draw_ensemble(key, part):
    keys = jax.random.split(jax.random.fold_in(key, 303), 3)
    full_shape = (MEMBERS, FIELDS, LEVELS, ROWS, COLS)
    amplitude = jax.random.uniform(keys[2], (1, FIELDS, LEVELS, ROWS, COLS), jnp.float32, 0.5, 1.5)
    noise = jnp.clip(jax.random.normal(keys[0], full_shape, jnp.float32), -4.0, 4.0)
    common = jnp.clip(jax.random.normal(keys[1], (MEMBERS, FIELDS, 1, 1, 1), jnp.float32), -3.0, 3.0)
    return noise + common * amplitude


def shard_levels(own_key, dims, cuts, least, largest):
    level = 1.0
    for dim, shards_of in cuts:
        steps = jax.random.uniform(jax.random.fold_in(jax.random.fold_in(own_key, 6), dim), (shards_of,), jnp.float32, least / len(cuts), largest / len(cuts))
        level = level * jnp.repeat(jnp.exp(steps), dims[dim] // shards_of).reshape((-1,) + (1,) * (len(dims) - 1 - dim))
    return level


def centred(rng, dims, scale, most, kind=jnp.bfloat16):
    array = jax.random.normal(rng, dims, jnp.float32) * scale
    return jnp.minimum(jnp.maximum(array, -most), most).astype(kind)


def setup_inputs(seed: int = 0) -> dict:
    splits = jax.random.split(jax.random.key(seed), 9)
    ensemble = draw_ensemble(jax.random.fold_in(splits[8], 71), 0)
    velocity = jnp.clip(jax.random.uniform(splits[1], (2, LEVELS, ROWS, COLS), jnp.float32, -0.5, 0.5) * shard_levels(splits[1], (2, LEVELS, ROWS, COLS), ((3, 16),), -0.4, 0.0), -0.5, 0.5)
    diffusivity = jnp.clip(jnp.exp(jax.random.uniform(splits[2], (FIELDS,), jnp.float32, math.log(0.05), math.log(0.2))), 0.05, 0.2)
    land_mask = draw_land_mask(jax.random.fold_in(splits[8], 71), 0)
    obs_index = draw_obs_index(jax.random.fold_in(splits[8], 71), 0)
    obs_owner = draw_obs_owner(jax.random.fold_in(splits[8], 71), 0)
    obs_value = centred(splits[6], (BATCHES, OBS_BATCH), 1.0, 4.0, jnp.float32)
    obs_error = jnp.clip(jnp.exp(jax.random.uniform(splits[7], (BATCHES, OBS_BATCH), jnp.float32, math.log(0.2), math.log(1.0))), 0.2, 1.0)
    return dict(ensemble=ensemble, velocity=velocity, diffusivity=diffusivity, land_mask=land_mask, obs_index=obs_index, obs_owner=obs_owner, obs_value=obs_value, obs_error=obs_error)


def gaspari(distance, loc_radius):
    scaled = distance / loc_radius
    scaled_safe = jnp.maximum(scaled, 1.0)
    near_part = (((-0.25 * scaled + 0.5) * scaled + 0.625) * scaled - 5.0 / 3.0) * scaled * scaled + 1.0
    far_part = ((((scaled / 12.0 - 0.5) * scaled + 0.625) * scaled + 5.0 / 3.0) * scaled - 5.0) * scaled + 4.0 - 2.0 / (3.0 * scaled_safe)
    return jnp.where(scaled <= 1.0, near_part, jnp.where(scaled < 2.0, far_part, 0.0))

def separation(row_from, col_from, row_to, col_to, grid_width):
    col_gap = jnp.abs(col_from - col_to)
    col_gap = jnp.minimum(col_gap, grid_width - col_gap)
    row_gap = row_from - row_to
    return jnp.sqrt((col_gap * col_gap + row_gap * row_gap).astype(jnp.float32))

def advance(center, col_next, col_prev, row_next, row_prev, flow_u, flow_v, diffuse, wet_part):
    tendency = -flow_u * (col_next - col_prev) * 0.5 - flow_v * (row_next - row_prev) * 0.5 + diffuse * (col_next + col_prev + row_next + row_prev - 4.0 * center)
    return wet_part * (center + tendency)

def reference(ensemble, velocity, diffusivity, land_mask, obs_index, obs_owner, obs_value, obs_error):
    wet_all = land_mask.astype(jnp.float32)
    col_next = jnp.roll(ensemble, -1, axis=4)
    col_prev = jnp.roll(ensemble, 1, axis=4)
    zero_row = jnp.zeros_like(ensemble[:, :, :, :1, :])
    row_next = jnp.concatenate([ensemble[:, :, :, 1:, :], zero_row], axis=3)
    row_prev = jnp.concatenate([zero_row, ensemble[:, :, :, :-1, :]], axis=3)
    diffuse = diffusivity[None, :, None, None, None]
    current = advance(ensemble, col_next, col_prev, row_next, row_prev, velocity[0][None, None], velocity[1][None, None], diffuse, wet_all)
    levels_total = FIELDS * LEVELS
    flat_state = current.reshape(MEMBERS, -1)
    wet_cells = wet_all.reshape(-1)
    wet_flat = jnp.broadcast_to(wet_all[None], (levels_total, ROWS, COLS)).reshape(-1)
    wet_count = jnp.sum(wet_cells)
    grid_rows = jnp.arange(ROWS, dtype=jnp.int32)[:, None]
    grid_cols = jnp.arange(COLS, dtype=jnp.int32)[None, :]
    spread = jnp.float32(MEMBERS - 1)
    loc_radius = float(LOC_RADIUS)
    for batch_num in range(BATCHES):
        obs_slot = obs_index[batch_num]
        owner_dev = obs_owner[batch_num]
        obs_rows = owner_dev // N_DOMAIN * ROWS_DEV + obs_slot[:, 2]
        obs_cols = owner_dev % N_DOMAIN * COLS_DEV + obs_slot[:, 3]
        level_of = obs_slot[:, 0] * LEVELS + obs_slot[:, 1]
        position = (level_of * ROWS + obs_rows) * COLS + obs_cols
        priors = jnp.take(flat_state, position.astype(jnp.int32), axis=1).T
        mutual = gaspari(separation(obs_rows[:, None], obs_cols[:, None], obs_rows[None, :], obs_cols[None, :], COLS), loc_radius)
        before = flat_state
        for obs_num in range(OBS_BATCH):
            prior_row = priors[obs_num]
            mean_prior = jnp.mean(prior_row)
            anomaly = prior_row - mean_prior
            obs_var = obs_error[batch_num, obs_num]
            denominator = jnp.sum(anomaly * anomaly) / spread + obs_var
            shrink = 1.0 / (1.0 + jnp.sqrt(obs_var / denominator))
            weight = obs_value[batch_num, obs_num] - mean_prior - shrink * anomaly
            taper = gaspari(separation(grid_rows, grid_cols, obs_rows[obs_num], obs_cols[obs_num], COLS), loc_radius)
            taper_flat = jnp.broadcast_to(taper[None], (levels_total, ROWS, COLS)).reshape(-1) * wet_flat
            covariance = jnp.dot(anomaly, flat_state, precision=lax.Precision.HIGHEST)
            kalman = taper_flat * covariance / (spread * denominator)
            flat_state = flat_state + weight[:, None] * kalman[None, :]
            prior_cov = jnp.dot(priors, anomaly, precision=lax.Precision.HIGHEST)
            priors = priors + (mutual[obs_num] * prior_cov / (spread * denominator))[:, None] * weight[None, :]
        change = lax.optimization_barrier(jnp.sum((flat_state - before).reshape(MEMBERS, levels_total, -1), axis=0))
        total_inc = lax.optimization_barrier(jnp.sum(change * wet_cells[None, :], axis=1))
        offset = total_inc / (MEMBERS * wet_count)
        flat_state = (flat_state.reshape(MEMBERS, levels_total, -1) - offset[None, :, None] * wet_cells[None, None, :]).reshape(MEMBERS, -1)
    return flat_state.reshape(MEMBERS, FIELDS, LEVELS, ROWS, COLS)
```

```python
import jax
import jax.numpy as jnp
from jax import lax
from jax.experimental import pallas as pl
from jax.experimental.pallas import tpu as pltpu
from jax.sharding import PartitionSpec as P

LOC_RADIUS = 64.0
MEM, DOM = 8, 16
MESH = pl.DeviceIdType.MESH
F32, BF16 = jnp.float32, jnp.bfloat16
HIGH = lax.Precision.HIGHEST


def gaspari(distance):
    scaled = distance * (1.0 / LOC_RADIUS)
    safe = jnp.maximum(scaled, 1.0)
    near = (((-0.25 * scaled + 0.5) * scaled + 0.625) * scaled - 5.0 / 3.0) * scaled * scaled + 1.0
    far = (
        ((((scaled * (1.0 / 12.0) - 0.5) * scaled + 0.625) * scaled + 5.0 / 3.0) * scaled - 5.0) * scaled
        + 4.0
        - (2.0 / 3.0) / safe
    )
    return jnp.where(scaled <= 1.0, near, jnp.where(scaled < 2.0, far, 0.0))


def separation(row_a, col_a, row_b, col_b):
    gap = jnp.abs(col_a - col_b)
    gap = jnp.minimum(gap, 4096 - gap)
    rows = row_a - row_b
    return jnp.sqrt((gap * gap + rows * rows).astype(F32))


def iota(shape, dim):
    return lax.broadcasted_iota(jnp.int32, shape, dim)


def halves(x):
    hi = x.astype(BF16)
    return hi, (x - hi.astype(F32)).astype(BF16)


def mm(a, b):
    return jnp.dot(a, b, preferred_element_type=F32)


def mm_nt(a, b, precision=None):
    return lax.dot_general(a, b, (((1,), (1,)), ((), ())), precision=precision, preferred_element_type=F32)


def kernel(
    ens, vel, mask, diff_in, oidx_in, oown_in, oval_in, oerr_in, x1_out, mrow_out,
    diff, oidx, oown, oval, oerr, E, V, W, F, D, eW, eE, pack, halo, vbuf, vin, Z, RB, TP, Pm, Zi, bcol, gcol, LB,
    L1h, L1l, L2h, L2l, Kf, Kh, Kl, sbuf, sin1, sin2,
    in_sem, loc_sem, out_sem, hs, hr, as_, ar, d1s, d1r, m1s, m1r, d2s, d2r, m2s, m2r,
):
    me, dom = lax.axis_index("member"), lax.axis_index("domain")

    small = ((vel, V), (mask, W), (diff_in, diff), (oidx_in, oidx), (oown_in, oown), (oval_in, oval), (oerr_in, oerr))
    small = [pltpu.make_async_copy(src, dst, in_sem.at[3 + i]) for i, (src, dst) in enumerate(small)]
    copies = []
    for g in range(3):
        copies.append(pltpu.make_async_copy(ens.at[:, pl.ds(4 * g, 4)], E.at[:, pl.ds(4 * g, 4)], in_sem.at[g]))
    for c in small + copies:
        c.start()
    barrier = pltpu.get_barrier_semaphore()
    for i in range(1, MEM):
        pl.semaphore_signal(barrier, inc=1, device_id={"member": lax.rem(me + i, MEM)}, device_id_type=MESH)
    for i in range(1, DOM):
        pl.semaphore_signal(barrier, inc=1, device_id={"domain": lax.rem(dom + i, DOM)}, device_id_type=MESH)
    for c in small:
        c.wait()

    wet = W[...].astype(F32)
    row, col = iota((16, 256), 0), iota((16, 256), 1)
    lane16 = iota((16, 128), 1)

    def interior(fl, acc):
        acc = list(acc)
        lev, fld = lax.rem(fl, 3), lax.div(fl, 3)
        u, v, d = V[0, lev], V[1, lev], diff[fld]
        cen = wet * (1.0 - 4.0 * d)
        east, west = wet * (d - 0.5 * u), wet * (d + 0.5 * u)
        north, south = wet * (d - 0.5 * v), wet * (d + 0.5 * v)
        eW[fl] = jnp.where(lane16 == 0, west[:, :128], 0.0)
        eE[fl] = jnp.where(lane16 == 127, east[:, 128:], 0.0)
        east, west = jnp.where(col == 255, 0.0, east), jnp.where(col == 0, 0.0, west)
        north, south = jnp.where(row == 15, 0.0, north), jnp.where(row == 0, 0.0, south)
        for m in range(10):
            x = E[m, fl]
            F[m, fl] = (
                cen * x
                + east * pltpu.roll(x, 255, 1)
                + west * pltpu.roll(x, 1, 1)
                + north * pltpu.roll(x, 15, 0)
                + south * pltpu.roll(x, 1, 0)
            )
            slot = 2 * ((m % 5) * 12 + fl)
            edges = pltpu.roll(jnp.where(lane16 == 0, x[:, :128], x[:, 128:]), slot, 1)
            here = (lane16 == slot) | (lane16 == jnp.bitwise_and(slot + 127, 127))
            acc[m // 5] = jnp.where(here, edges, acc[m // 5])
        return tuple(acc)

    acc = (jnp.zeros((16, 128), F32), jnp.zeros((16, 128), F32))
    for g in range(3):
        copies[g].wait()
        acc = lax.fori_loop(4 * g, 4 * g + 4, interior, acc)
    pack[0], pack[1] = acc[0], acc[1]

    lane32, sub32 = iota((32, 128), 1), iota((32, 128), 0)

    def wide_l(x, rows):
        return jnp.broadcast_to(x[0:1, :], (rows, 128))

    zi = jnp.zeros((32, 128), jnp.int32)
    row_s, col_s, fl_s, row_l, col_l, fl_l = zi, zi, zi, zi, zi, zi
    val_s = jnp.zeros((32, 128), F32)
    places = []
    for k in range(32):
        b, n = k // 8, k % 8
        own = oown[b]
        r = jnp.right_shift(own, 4) * 2 + oidx[b, 2, n]
        c = jnp.bitwise_and(own, 15) * 256 + oidx[b, 3, n]
        f = oidx[b, 0, n] * 3 + oidx[b, 1, n]
        places.append((r, c))
        row_s, col_s, fl_s = (jnp.where(sub32 == k, s, a) for s, a in ((r, row_s), (c, col_s), (f, fl_s)))
        row_l, col_l, fl_l = (jnp.where(lane32 == k, s, a) for s, a in ((r, row_l), (c, col_l), (f, fl_l)))
        val_s = jnp.where(sub32 == k, oval[b, n], val_s)
    rho = gaspari(separation(row_s, col_s, row_l, col_l))
    for k in range(32):
        RB[k] = jnp.broadcast_to(rho[:, k : k + 1], (32, 128))

    sub8, lane8 = iota((8, 256), 0), iota((8, 256), 1)
    odd = jnp.bitwise_and(sub8, 1) == 1
    wet0 = jnp.broadcast_to(W[pl.ds(2 * me, 1), :].astype(F32), (8, 256))
    wet1 = jnp.broadcast_to(W[pl.ds(2 * me + 1, 1), :].astype(F32), (8, 256))
    wet8 = jnp.where(odd, wet1, wet0)
    row8, col8 = 2 * me + jnp.bitwise_and(sub8, 1), dom * 256 + lane8
    for k in range(32):
        TP[k] = gaspari(separation(row8, col8, places[k][0], places[k][1])) * wet8

    pl.semaphore_wait(barrier, MEM + DOM - 2)

    right, left = lax.rem(dom + 1, DOM), lax.rem(dom + DOM - 1, DOM)
    sends = []

    def remote(src, dst, send, recv, where):
        c = pltpu.make_async_remote_copy(
            src_ref=src, dst_ref=dst, send_sem=send, recv_sem=recv, device_id=where, device_id_type=MESH
        )
        c.start()
        sends.append(c)
        return c

    to_left = remote(pack, halo.at[0], hs.at[0], hr.at[0], {"domain": left})
    to_right = remote(pack, halo.at[1], hs.at[1], hr.at[1], {"domain": right})
    to_left.wait_recv()
    to_right.wait_recv()
    even = jnp.bitwise_and(lane16, 1) == 0
    merged = [jnp.where(even, halo[0, h], pltpu.roll(halo[1, h], 2, 1)) for h in range(2)]

    def fix(fl, carry):
        west, east = eW[fl], eE[fl]
        for m in range(10):
            slot = 2 * ((m % 5) * 12 + fl)
            y = pltpu.roll(merged[m // 5], 127 - slot, 1)
            F[m, fl, :, 0:128] = F[m, fl, :, 0:128] + y * west
            F[m, fl, :, 128:256] = F[m, fl, :, 128:256] + y * east
        return carry

    arrivals, locals_ = [], []

    def scatter(g):
        fls = pl.ds(4 * g, 4)
        mine = D.at[pl.ds(10 * lax.div(me, 4), 10), fls, pl.ds(2 * lax.rem(me, 4), 2), :]
        c = pltpu.make_async_copy(F.at[:, fls, pl.ds(2 * me, 2), :], mine, loc_sem.at[g])
        c.start()
        locals_.append(c)
        for i in (4, 5, 3, 2, 6, 1, 7):
            t = lax.rem(me + i, MEM)
            arrivals.append(
                remote(F.at[:, fls, pl.ds(2 * t, 2), :], mine, as_.at[7 * g + i - 1], ar.at[7 * g + i - 1], {"member": t})
            )

    lax.fori_loop(0, 4, fix, 0)
    scatter(0)
    lax.fori_loop(4, 12, fix, 0)

    pick = (iota((256, 128), 0) + dom * 256 == wide_l(col_l, 256)) & (iota((256, 128), 1) < 32)
    pick = jnp.where(pick, 1.0, 0.0).astype(BF16)
    at_row = jnp.bitwise_and(iota((160, 128), 0), 15) == wide_l(row_l, 160)
    got = jnp.zeros((160, 128), F32)
    for fl in range(12):
        x = F[:, fl].reshape(160, 256)
        hi = x.astype(BF16)
        rest = x - hi.astype(F32)
        mid, lo = halves(rest)
        got = jnp.where(wide_l(fl_l, 160) == fl, mm(hi, pick) + (mm(mid, pick) + mm(lo, pick)), got)
    got = jnp.where(at_row, got, 0.0)
    vbuf[...] = jnp.zeros((16, 128), F32)
    vbuf[0:10, :] = jnp.sum(got.reshape(10, 16, 128), axis=1)
    tile_parts = [
        remote(vbuf, vin.at[i - 1], d1s.at[i - 1], d1r.at[i - 1], {"domain": lax.rem(dom + i, DOM)}) for i in range(1, DOM)
    ]
    scatter(1)
    scatter(2)
    total = vbuf[...]
    for i, c in enumerate(tile_parts):
        c.wait_recv()
        total = total + vin[i]
    Z[me] = total
    groups = [
        remote(Z.at[me], Z.at[me], m1s.at[i - 1], m1r.at[i - 1], {"member": lax.rem(me + i, MEM)}) for i in range(1, MEM)
    ]
    for c in groups:
        c.wait_recv()

    Y = jnp.transpose(Z[...].reshape(128, 128))[:32]
    real = jnp.bitwise_and(lane32, 15) < 10
    ybar = jnp.broadcast_to(jnp.sum(Y, axis=1, keepdims=True) * (1.0 / 80.0), (32, 128))
    A = jnp.where(real, Y - ybar, 0.0)
    inv = jnp.where(lane32 == sub32, 1.0, 0.0).astype(F32)
    for k in range(32):
        a, z = A[k : k + 1, :], inv[k : k + 1, :]
        cov = jnp.broadcast_to(jnp.sum(A * a, axis=1, keepdims=True), (32, 128))
        err = oerr[k // 8, k % 8]
        den = cov[k : k + 1, :] * (1.0 / 79.0) + err
        gain = 1.0 / (79.0 * den)
        beta = 1.0 / (1.0 + jnp.sqrt(err / den))
        Pm[k : k + 1, :] = a
        Zi[k : k + 1, :] = z
        bcol[k : k + 1, :] = beta
        gcol[k : k + 1, :] = gain
        step = RB[k] * cov * gain
        A = A - (step * beta) * a
        inv = inv - step * z

    Pv = Pm[...]
    Pb = Pv * bcol[...]
    low = mm_nt(Pv, Pb, HIGH)
    for j in range(31):
        LB[j] = jnp.broadcast_to(low[:, j : j + 1], (32, 128))
    for k in range(32):
        TP[k] = TP[k] * jnp.broadcast_to(gcol[k : k + 1, 0:1], (8, 256))

    n = iota((128, 640), 1)
    unit = jnp.right_shift(n, 5)
    q = jnp.bitwise_and(jnp.right_shift(n, 1), 3)
    upper = (unit >= 10).astype(jnp.int32)
    spread = jnp.where((4 * upper + q) * 16 + unit - 10 * upper == iota((128, 640), 0), 1.0, 0.0).astype(BF16)
    n = iota((8, 640), 1)
    match = jnp.bitwise_and(jnp.right_shift(n, 3), 3) * 2 + jnp.bitwise_and(n, 1) == iota((8, 640), 0)
    keep = jnp.broadcast_to(jnp.where(match, 1.0, 0.0)[None], (32, 8, 640))

    def kron(part):
        return (jnp.broadcast_to(mm(part, spread)[:, None, :], (32, 8, 640)) * keep).reshape(256, 640)

    hi, lo = halves(Pv)
    L1h[...] = kron(hi).astype(BF16)
    L1l[...] = kron(lo).astype(BF16)
    hi, lo = halves(Pb)
    L2h[...] = jnp.transpose(kron(hi)).astype(BF16)
    L2l[...] = jnp.transpose(kron(lo)).astype(BF16)
    invT = jnp.transpose(jnp.concatenate([Zi[...], jnp.zeros((96, 128), F32)], axis=0))[:32]

    sums = jnp.zeros((8, 256), F32)
    for g in range(3):
        locals_[g].wait()
        for c in arrivals[7 * g : 7 * g + 7]:
            c.wait_recv()
        xh, xl = halves(D[:, 4 * g : 4 * g + 4].reshape(640, 256))
        cov = mm(L1h[...], xh) + (mm(L1h[...], xl) + mm(L1l[...], xh))
        gains = []
        for k in range(32):
            left_, right_ = cov[8 * k : 8 * k + 8, :128], cov[8 * k : 8 * k + 8, 128:]
            for j in range(k):
                s = jnp.broadcast_to(LB[j, k : k + 1, :], (8, 128))
                left_, right_ = left_ - s * gains[j][0], right_ - s * gains[j][1]
            left_, right_ = left_ * TP[k, :, 0:128], right_ * TP[k, :, 128:256]
            gains.append((left_, right_))
            Kf[g, 8 * k : 8 * k + 8, 0:128] = left_
            Kf[g, 8 * k : 8 * k + 8, 128:256] = right_
        hi, lo = halves(Kf[g])
        Kh[g], Kl[g] = hi, lo
        pick = jnp.where(sub8 == g, 1.0, 0.0).astype(BF16)
        sums = sums + (mm_nt(pick, hi) + mm_nt(pick, lo))
    sbuf[0] = jnp.where(sub8 == 3, wet0 + wet1, sums)
    parts = [
        remote(sbuf.at[0], sin1.at[i - 1], d2s.at[i - 1], d2r.at[i - 1], {"domain": lax.rem(dom + i, DOM)})
        for i in range(1, DOM)
    ]

    outs = []

    def update(g):
        change = mm(L2h[...], Kh[g]) + (mm(L2h[...], Kl[g]) + mm(L2l[...], Kh[g]))
        D[:, 4 * g : 4 * g + 4] = D[:, 4 * g : 4 * g + 4] - change.reshape(20, 4, 8, 256)
        for s in range(8):
            c = pltpu.make_async_copy(
                D.at[pl.ds(10 * (s // 4), 10), pl.ds(4 * g, 4), pl.ds(2 * (s % 4), 2), :],
                x1_out.at[pl.ds(10 * s, 10), pl.ds(4 * g, 4), :, :],
                out_sem.at[8 * g + s],
            )
            c.start()
            outs.append(c)

    update(0)
    update(1)
    total = sbuf[0]
    for i, c in enumerate(parts):
        c.wait_recv()
        total = total + sin1[i]
    sbuf[1] = total
    parts = [
        remote(sbuf.at[1], sin2.at[i - 1], m2s.at[i - 1], m2r.at[i - 1], {"member": lax.rem(me + i, MEM)})
        for i in range(1, MEM)
    ]
    update(2)
    for i, c in enumerate(parts):
        c.wait_recv()
        total = total + sin2[i]

    cells = jnp.sum(jnp.sum(jnp.where(sub8 == 3, total, 0.0), axis=1, keepdims=True), axis=0, keepdims=True)
    share = total * (1.0 / jnp.broadcast_to(cells, (8, 256)))
    fl_w = jnp.concatenate([fl_s, fl_s], axis=1)
    picked = jnp.zeros((32, 256), F32)
    for g in range(3):
        picked = jnp.where(jnp.right_shift(fl_w, 2) == g, share[g : g + 1, :], picked)
    four = jnp.bitwise_and(jnp.right_shift(iota((32, 256), 1), 1), 3)
    picked = jnp.where(four == jnp.bitwise_and(fl_w, 3), picked, 0.0)
    fold = jnp.where(jnp.right_shift(iota((256, 128), 0), 3) == iota((256, 128), 1), 1.0, 0.0).astype(BF16)
    hi, lo = halves(picked)
    shifts = mm(hi, fold) + mm(lo, fold)
    shifts = jnp.where(jnp.right_shift(lane32, 3) < jnp.right_shift(sub32, 3), shifts, 0.0)
    base = val_s - ybar
    innov = jnp.sum(invT * base, axis=0, keepdims=True)
    for _ in range(3):
        moved = base + jnp.sum(shifts * innov, axis=1, keepdims=True)
        innov = jnp.sum(invT * moved, axis=0, keepdims=True)
    wide = jnp.zeros((8, 256), F32)
    mean = [jnp.zeros((8, 256), F32) for _ in range(3)]
    for k in range(32):
        dk = jnp.broadcast_to(innov[0:1, k : k + 1], (8, 256))
        wide = jnp.where(jnp.right_shift(lane8, 3) == k, dk, wide)
        mean = [mean[g] + dk * Kf[g, 8 * k : 8 * k + 8, :] for g in range(3)]
    same = jnp.bitwise_and(jnp.right_shift(lane8, 1), 3) == jnp.right_shift(sub8, 1)
    for g in range(3):
        part = jnp.where(same, share[g : g + 1, :] * wide, 0.0)
        shift = jnp.broadcast_to(jnp.sum(part, axis=1, keepdims=True), (8, 256))
        mrow_out[8 * g : 8 * g + 8, :] = mean[g] - wet8 * shift
    for c in outs:
        c.wait()
    for c in sends:
        c.wait_send()


def local(ensemble, velocity, diffusivity, land_mask, obs_index, obs_owner, obs_value, obs_error):
    hbm = pl.BlockSpec(memory_space=pltpu.HBM)
    vm = lambda *shape, t=F32: pltpu.VMEM(shape, t)
    dma = lambda n: pltpu.SemaphoreType.DMA((n,))
    x1, mrow = pl.pallas_call(
        kernel,
        out_shape=(jax.ShapeDtypeStruct((80, 12, 2, 256), F32), jax.ShapeDtypeStruct((24, 256), F32)),
        in_specs=[hbm] * 8,
        out_specs=(pl.BlockSpec(memory_space=pl.ANY), pl.BlockSpec(memory_space=pltpu.VMEM)),
        scratch_shapes=[
            pltpu.SMEM((4,), F32), pltpu.SMEM((4, 4, 8), jnp.int32), pltpu.SMEM((4,), jnp.int32),
            pltpu.SMEM((4, 8), F32), pltpu.SMEM((4, 8), F32),
            vm(10, 12, 16, 256), vm(2, 3, 16, 256), vm(16, 256, t=jnp.int32), vm(10, 12, 16, 256),
            vm(20, 12, 8, 256), vm(12, 16, 128), vm(12, 16, 128), vm(2, 16, 128), vm(2, 2, 16, 128),
            vm(16, 128), vm(15, 16, 128), vm(8, 16, 128), vm(32, 32, 128), vm(32, 8, 256),
            vm(32, 128), vm(32, 128), vm(32, 128), vm(32, 128), vm(32, 32, 128),
            vm(256, 640, t=BF16), vm(256, 640, t=BF16), vm(640, 256, t=BF16), vm(640, 256, t=BF16),
            vm(3, 256, 256), vm(3, 256, 256, t=BF16), vm(3, 256, 256, t=BF16),
            vm(2, 8, 256), vm(15, 8, 256), vm(7, 8, 256),
            dma(10), dma(3), dma(24), dma(2), dma(2), dma(21), dma(21),
            dma(15), dma(15), dma(7), dma(7), dma(15), dma(15), dma(7), dma(7),
        ],
        compiler_params=pltpu.CompilerParams(collective_id=0, has_side_effects=True, vmem_limit_bytes=58 << 20),
    )(
        ensemble.reshape(10, 12, 16, 256),
        velocity,
        land_mask,
        diffusivity,
        jnp.transpose(obs_index, (0, 2, 1)),
        obs_owner,
        obs_value,
        obs_error,
    )
    return (x1 + mrow.reshape(1, 12, 2, 256)).reshape(80, 4, 3, 2, 256)


def solution(mesh):
    in_specs = (
        P("member", None, None, None, "domain"),
        P(None, None, None, "domain"),
        P(),
        P(None, "domain"),
        P(),
        P(),
        P(),
        P(),
    )
    out_specs = P(None, None, None, "member", "domain")
    return jax.shard_map(local, mesh=mesh, in_specs=in_specs, out_specs=out_specs, check_vma=False)
```

```python
import jax
import jax.numpy as jnp
from jax import lax
from jax.experimental import pallas as pl
from jax.experimental.pallas import tpu as pltpu
from jax.sharding import PartitionSpec as P

LOC_RADIUS = 64.0
MEM, DOM = 8, 16
MESH = pl.DeviceIdType.MESH
F32, BF16 = jnp.float32, jnp.bfloat16
HIGH = lax.Precision.HIGHEST


def gaspari(distance):
    scaled = distance * (1.0 / LOC_RADIUS)
    safe = jnp.maximum(scaled, 1.0)
    near = (((-0.25 * scaled + 0.5) * scaled + 0.625) * scaled - 5.0 / 3.0) * scaled * scaled + 1.0
    far = (
        ((((scaled * (1.0 / 12.0) - 0.5) * scaled + 0.625) * scaled + 5.0 / 3.0) * scaled - 5.0) * scaled
        + 4.0
        - (2.0 / 3.0) / safe
    )
    return jnp.where(scaled <= 1.0, near, jnp.where(scaled < 2.0, far, 0.0))


def separation(row_a, col_a, row_b, col_b):
    gap = jnp.abs(col_a - col_b)
    gap = jnp.minimum(gap, 4096 - gap)
    rows = row_a - row_b
    return jnp.sqrt((gap * gap + rows * rows).astype(F32))


def iota(shape, dim):
    return lax.broadcasted_iota(jnp.int32, shape, dim)


def halves(x):
    hi = x.astype(BF16)
    return hi, (x - hi.astype(F32)).astype(BF16)


def mm(a, b):
    return jnp.dot(a, b, preferred_element_type=F32)


def mm_nt(a, b, precision=None):
    return lax.dot_general(a, b, (((1,), (1,)), ((), ())), precision=precision, preferred_element_type=F32)


def kernel(
    ens, vel, mask, diff_in, oidx_in, oown_in, oval_in, oerr_in, x1_out, mrow_out,
    diff, oidx, oown, oval, oerr, E, V, W, F, D, pack, halo, corr, CR, vbuf, vin, Z, RB, TP, Pm, Zi, bcol, gcol, LB,
    L1h, L1l, L2h, L2l, Kf, Kh, Kl, sbuf, sin1, sin2, M,
    in_sem, loc_sem, out_sem, hs, hr, cs, cr, as_, ar, d1s, d1r, m1s, m1r, d2s, d2r, m2s, m2r,
):
    me, dom = lax.axis_index("member"), lax.axis_index("domain")

    small = ((vel, V), (mask, W), (diff_in, diff), (oidx_in, oidx), (oown_in, oown), (oval_in, oval), (oerr_in, oerr))
    small = [pltpu.make_async_copy(src, dst, in_sem.at[3 + i]) for i, (src, dst) in enumerate(small)]
    copies = []
    for g in range(3):
        copies.append(pltpu.make_async_copy(ens.at[:, pl.ds(4 * g, 4)], E.at[:, pl.ds(4 * g, 4)], in_sem.at[g]))
    for c in small + copies:
        c.start()
    barrier = pltpu.get_barrier_semaphore()
    for i in range(1, MEM):
        pl.semaphore_signal(barrier, inc=1, device_id={"member": lax.rem(me + i, MEM)}, device_id_type=MESH)
    for i in range(1, DOM):
        pl.semaphore_signal(barrier, inc=1, device_id={"domain": lax.rem(dom + i, DOM)}, device_id_type=MESH)
    for c in small:
        c.wait()

    wet = W[...].astype(F32)
    row, col = iota((16, 256), 0), iota((16, 256), 1)
    lane16 = iota((16, 128), 1)
    even = jnp.bitwise_and(lane16, 1) == 0
    slot_fl = jnp.right_shift(lane16, 1)
    for _ in range(4):
        slot_fl = jnp.where(slot_fl >= 12, slot_fl - 12, slot_fl)
    slot_fl = jnp.where(lane16 < 120, slot_fl, -1)

    def interior(fl, acc):
        acc = list(acc)
        lev, fld = lax.rem(fl, 3), lax.div(fl, 3)
        u, v, d = V[0, lev], V[1, lev], diff[fld]
        cen = wet * (1.0 - 4.0 * d)
        east, west = wet * (d - 0.5 * u), wet * (d + 0.5 * u)
        north, south = wet * (d - 0.5 * v), wet * (d + 0.5 * v)
        ours = slot_fl == fl
        acc[2] = jnp.where(ours & even, jnp.broadcast_to(east[:, 255:256], (16, 128)), acc[2])
        acc[2] = jnp.where(ours & ~even, jnp.broadcast_to(west[:, 0:1], (16, 128)), acc[2])
        east, west = jnp.where(col == 255, 0.0, east), jnp.where(col == 0, 0.0, west)
        north, south = jnp.where(row == 15, 0.0, north), jnp.where(row == 0, 0.0, south)
        for m in range(10):
            x = E[m, fl]
            y = (
                cen * x
                + east * pltpu.roll(x, 255, 1)
                + west * pltpu.roll(x, 1, 1)
                + north * pltpu.roll(x, 15, 0)
                + south * pltpu.roll(x, 1, 0)
            )
            F[m, fl] = y
            E[m, fl] = y
            slot = 2 * ((m % 5) * 12 + fl)
            edges = pltpu.roll(jnp.where(lane16 == 0, x[:, :128], x[:, 128:]), slot, 1)
            here = (lane16 == slot) | (lane16 == jnp.bitwise_and(slot + 127, 127))
            acc[m // 5] = jnp.where(here, edges, acc[m // 5])
        return tuple(acc)

    acc = tuple(jnp.zeros((16, 128), F32) for _ in range(3))
    for g in range(3):
        copies[g].wait()
        acc = lax.fori_loop(4 * g, 4 * g + 4, interior, acc)
    pack[0], pack[1] = acc[0], acc[1]

    lane32, sub32 = iota((32, 128), 1), iota((32, 128), 0)

    def wide_l(x, rows):
        return jnp.broadcast_to(x[0:1, :], (rows, 128))

    zi = jnp.zeros((32, 128), jnp.int32)
    row_s, col_s, fl_s, row_l, col_l, fl_l = zi, zi, zi, zi, zi, zi
    val_s = jnp.zeros((32, 128), F32)
    places = []
    for k in range(32):
        b, n = k // 8, k % 8
        own = oown[b]
        r = jnp.right_shift(own, 4) * 2 + oidx[b, 2, n]
        c = jnp.bitwise_and(own, 15) * 256 + oidx[b, 3, n]
        f = oidx[b, 0, n] * 3 + oidx[b, 1, n]
        places.append((r, c))
        row_s, col_s, fl_s = (jnp.where(sub32 == k, s, a) for s, a in ((r, row_s), (c, col_s), (f, fl_s)))
        row_l, col_l, fl_l = (jnp.where(lane32 == k, s, a) for s, a in ((r, row_l), (c, col_l), (f, fl_l)))
        val_s = jnp.where(sub32 == k, oval[b, n], val_s)
    rho = gaspari(separation(row_s, col_s, row_l, col_l))
    for k in range(32):
        RB[k] = jnp.broadcast_to(rho[:, k : k + 1], (32, 128))

    sub8, lane8 = iota((8, 256), 0), iota((8, 256), 1)
    odd = jnp.bitwise_and(sub8, 1) == 1
    wet0 = jnp.broadcast_to(W[pl.ds(2 * me, 1), :].astype(F32), (8, 256))
    wet1 = jnp.broadcast_to(W[pl.ds(2 * me + 1, 1), :].astype(F32), (8, 256))
    wet8 = jnp.where(odd, wet1, wet0)
    row8, col8 = 2 * me + jnp.bitwise_and(sub8, 1), dom * 256 + lane8
    for k in range(32):
        TP[k] = gaspari(separation(row8, col8, places[k][0], places[k][1])) * wet8

    pl.semaphore_wait(barrier, MEM + DOM - 2)

    right, left = lax.rem(dom + 1, DOM), lax.rem(dom + DOM - 1, DOM)
    sends = []

    def remote(src, dst, send, recv, where):
        c = pltpu.make_async_remote_copy(
            src_ref=src, dst_ref=dst, send_sem=send, recv_sem=recv, device_id=where, device_id_type=MESH
        )
        c.start()
        sends.append(c)
        return c

    to_left = remote(pack, halo.at[0], hs.at[0], hr.at[0], {"domain": left})
    to_right = remote(pack, halo.at[1], hs.at[1], hr.at[1], {"domain": right})

    arrivals, locals_ = [], []
    own_rows, own_slot = pl.ds(2 * me, 2), pl.ds(2 * lax.rem(me, 4), 2)
    half = lax.div(me, 4)

    def scatter(g):
        fls = pl.ds(2 * g, 2)
        mine = D.at[pl.ds(10 * half, 10), fls, own_slot, :]
        c = pltpu.make_async_copy(F.at[:, fls, own_rows, :], mine, loc_sem.at[g])
        c.start()
        locals_.append(c)
        for i in (4, 5, 3, 2, 6, 1, 7):
            t = lax.rem(me + i, MEM)
            n = 7 * g + i - 1
            arrivals.append(remote(F.at[:, fls, pl.ds(2 * t, 2), :], mine, as_.at[n], ar.at[n], {"member": t}))

    scatter(0)
    scatter(1)

    to_left.wait_recv()
    to_right.wait_recv()
    for h in range(2):
        corr[h] = jnp.where(even, halo[0, h], pltpu.roll(halo[1, h], 2, 1)) * acc[2]
    fixes = []
    mine = CR.at[half, :, own_slot, :]
    own_corr = pltpu.make_async_copy(corr.at[:, own_rows, :], mine, loc_sem.at[6])
    own_corr.start()
    for i in (4, 5, 3, 2, 6, 1, 7):
        t = lax.rem(me + i, MEM)
        fixes.append(remote(corr.at[:, pl.ds(2 * t, 2), :], mine, cs.at[i - 1], cr.at[i - 1], {"member": t}))
    added = [corr[0], corr[1]]

    def fix(fl, carry):
        for m in range(10):
            y = pltpu.roll(added[m // 5], 127 - 2 * ((m % 5) * 12 + fl), 1)
            E[m, fl, :, 0:128] = E[m, fl, :, 0:128] + jnp.where(lane16 == 0, y, 0.0)
            E[m, fl, :, 128:256] = E[m, fl, :, 128:256] + jnp.where(lane16 == 127, y, 0.0)
        return carry

    lax.fori_loop(0, 12, fix, 0)

    pick = (iota((256, 128), 0) + dom * 256 == wide_l(col_l, 256)) & (iota((256, 128), 1) < 32)
    pick = jnp.where(pick, 1.0, 0.0).astype(BF16)
    at_row = jnp.bitwise_and(iota((160, 128), 0), 15) == wide_l(row_l, 160)
    got = jnp.zeros((160, 128), F32)
    for fl in range(12):
        x = E[:, fl].reshape(160, 256)
        hi = x.astype(BF16)
        rest = x - hi.astype(F32)
        mid, lo = halves(rest)
        got = jnp.where(wide_l(fl_l, 160) == fl, mm(hi, pick) + (mm(mid, pick) + mm(lo, pick)), got)
    got = jnp.where(at_row, got, 0.0)
    vbuf[...] = jnp.zeros((16, 128), F32)
    vbuf[0:10, :] = jnp.sum(got.reshape(10, 16, 128), axis=1)
    tile_parts = [
        remote(vbuf, vin.at[i - 1], d1s.at[i - 1], d1r.at[i - 1], {"domain": lax.rem(dom + i, DOM)}) for i in range(1, DOM)
    ]
    scatter(2)
    total = vbuf[...]
    for i, c in enumerate(tile_parts):
        c.wait_recv()
        total = total + vin[i]
    Z[me] = total
    groups = [
        remote(Z.at[me], Z.at[me], m1s.at[i - 1], m1r.at[i - 1], {"member": lax.rem(me + i, MEM)}) for i in range(1, MEM)
    ]
    scatter(3)
    scatter(4)
    scatter(5)
    for c in groups:
        c.wait_recv()

    Y = jnp.transpose(Z[...].reshape(128, 128))[:32]
    real = jnp.bitwise_and(lane32, 15) < 10
    ybar = jnp.broadcast_to(jnp.sum(Y, axis=1, keepdims=True) * (1.0 / 80.0), (32, 128))
    A = jnp.where(real, Y - ybar, 0.0)
    inv = jnp.where(lane32 == sub32, 1.0, 0.0).astype(F32)
    for k in range(32):
        a, z = A[k : k + 1, :], inv[k : k + 1, :]
        cov = jnp.broadcast_to(jnp.sum(A * a, axis=1, keepdims=True), (32, 128))
        err = oerr[k // 8, k % 8]
        den = cov[k : k + 1, :] * (1.0 / 79.0) + err
        gain = 1.0 / (79.0 * den)
        beta = 1.0 / (1.0 + jnp.sqrt(err / den))
        Pm[k : k + 1, :] = a
        Zi[k : k + 1, :] = z
        bcol[k : k + 1, :] = beta
        gcol[k : k + 1, :] = gain
        step = RB[k] * cov * gain
        A = A - (step * beta) * a
        inv = inv - step * z

    Pv = Pm[...]
    Pb = Pv * bcol[...]
    low = mm_nt(Pv, Pb, HIGH)
    for j in range(31):
        LB[j] = jnp.broadcast_to(low[:, j : j + 1], (32, 128))
    for k in range(32):
        TP[k] = TP[k] * jnp.broadcast_to(gcol[k : k + 1, 0:1], (8, 256))

    n = iota((128, 640), 1)
    unit = jnp.right_shift(n, 5)
    q = jnp.bitwise_and(jnp.right_shift(n, 1), 3)
    upper = (unit >= 10).astype(jnp.int32)
    spread = jnp.where((4 * upper + q) * 16 + unit - 10 * upper == iota((128, 640), 0), 1.0, 0.0).astype(BF16)
    n = iota((8, 640), 1)
    match = jnp.bitwise_and(jnp.right_shift(n, 3), 3) * 2 + jnp.bitwise_and(n, 1) == iota((8, 640), 0)
    keep = jnp.broadcast_to(jnp.where(match, 1.0, 0.0)[None], (32, 8, 640))

    def kron(part):
        return (jnp.broadcast_to(mm(part, spread)[:, None, :], (32, 8, 640)) * keep).reshape(256, 640)

    hi, lo = halves(Pv)
    L1h[...] = kron(hi).astype(BF16)
    L1l[...] = kron(lo).astype(BF16)
    hi, lo = halves(Pb)
    L2h[...] = jnp.transpose(kron(hi)).astype(BF16)
    L2l[...] = jnp.transpose(kron(lo)).astype(BF16)
    invT = jnp.transpose(jnp.concatenate([Zi[...], jnp.zeros((96, 128), F32)], axis=0))[:32]

    sums = jnp.zeros((8, 256), F32)
    own_corr.wait()
    for c in fixes:
        c.wait_recv()
    first, last = iota((8, 128), 1) == 0, iota((8, 128), 1) == 127

    def amend(fl, carry):
        for u in range(20):
            y = pltpu.roll(CR[u // 10, u % 10 // 5], 127 - 2 * ((u % 5) * 12 + fl), 1)
            D[u, fl, :, 0:128] = D[u, fl, :, 0:128] + jnp.where(first, y, 0.0)
            D[u, fl, :, 128:256] = D[u, fl, :, 128:256] + jnp.where(last, y, 0.0)
        return carry

    for g in range(3):
        for u in (2 * g, 2 * g + 1):
            locals_[u].wait()
            for c in arrivals[7 * u : 7 * u + 7]:
                c.wait_recv()
        lax.fori_loop(4 * g, 4 * g + 4, amend, 0)
        xh, xl = halves(D[:, 4 * g : 4 * g + 4].reshape(640, 256))
        cov = mm(L1h[...], xh) + (mm(L1h[...], xl) + mm(L1l[...], xh))
        gains = []
        for k in range(32):
            left_, right_ = cov[8 * k : 8 * k + 8, :128], cov[8 * k : 8 * k + 8, 128:]
            for j in range(k):
                s = jnp.broadcast_to(LB[j, k : k + 1, :], (8, 128))
                left_, right_ = left_ - s * gains[j][0], right_ - s * gains[j][1]
            left_, right_ = left_ * TP[k, :, 0:128], right_ * TP[k, :, 128:256]
            gains.append((left_, right_))
            Kf[g, 8 * k : 8 * k + 8, 0:128] = left_
            Kf[g, 8 * k : 8 * k + 8, 128:256] = right_
        hi, lo = halves(Kf[g])
        Kh[g], Kl[g] = hi, lo
        pick = jnp.where(sub8 == g, 1.0, 0.0).astype(BF16)
        sums = sums + (mm_nt(pick, hi) + mm_nt(pick, lo))
    sbuf[0] = jnp.where(sub8 == 3, wet0 + wet1, sums)
    parts = [
        remote(sbuf.at[0], sin1.at[i - 1], d2s.at[i - 1], d2r.at[i - 1], {"domain": lax.rem(dom + i, DOM)})
        for i in range(1, DOM)
    ]

    outs = []

    def update(g):
        change = mm(L2h[...], Kh[g]) + (mm(L2h[...], Kl[g]) + mm(L2l[...], Kh[g]))
        D[:, 4 * g : 4 * g + 4] = D[:, 4 * g : 4 * g + 4] - change.reshape(20, 4, 8, 256)
        for s in range(8):
            c = pltpu.make_async_copy(
                D.at[pl.ds(10 * (s // 4), 10), pl.ds(4 * g, 4), pl.ds(2 * (s % 4), 2), :],
                x1_out.at[pl.ds(10 * s, 10), pl.ds(4 * g, 4), :, :],
                out_sem.at[8 * g + s],
            )
            c.start()
            outs.append(c)

    update(0)
    update(1)
    total = sbuf[0]
    for i, c in enumerate(parts):
        c.wait_recv()
        total = total + sin1[i]
    sbuf[1] = total
    parts = [
        remote(sbuf.at[1], sin2.at[i - 1], m2s.at[i - 1], m2r.at[i - 1], {"member": lax.rem(me + i, MEM)})
        for i in range(1, MEM)
    ]
    update(2)
    for i, c in enumerate(parts):
        c.wait_recv()
        total = total + sin2[i]

    cells = jnp.sum(jnp.sum(jnp.where(sub8 == 3, total, 0.0), axis=1, keepdims=True), axis=0, keepdims=True)
    share = total * (1.0 / jnp.broadcast_to(cells, (8, 256)))
    fl_w = jnp.concatenate([fl_s, fl_s], axis=1)
    picked = jnp.zeros((32, 256), F32)
    for g in range(3):
        picked = jnp.where(jnp.right_shift(fl_w, 2) == g, share[g : g + 1, :], picked)
    four = jnp.bitwise_and(jnp.right_shift(iota((32, 256), 1), 1), 3)
    picked = jnp.where(four == jnp.bitwise_and(fl_w, 3), picked, 0.0)
    fold = jnp.where(jnp.right_shift(iota((256, 128), 0), 3) == iota((256, 128), 1), 1.0, 0.0).astype(BF16)
    hi, lo = halves(picked)
    shifts = mm(hi, fold) + mm(lo, fold)
    shifts = jnp.where(jnp.right_shift(lane32, 3) < jnp.right_shift(sub32, 3), shifts, 0.0)
    base = val_s - ybar
    innov = jnp.sum(invT * base, axis=0, keepdims=True)
    for _ in range(3):
        moved = base + jnp.sum(shifts * innov, axis=1, keepdims=True)
        innov = jnp.sum(invT * moved, axis=0, keepdims=True)
    wide = jnp.zeros((8, 256), F32)
    mean = [jnp.zeros((8, 256), F32) for _ in range(3)]
    for k in range(32):
        dk = jnp.broadcast_to(innov[0:1, k : k + 1], (8, 256))
        wide = jnp.where(jnp.right_shift(lane8, 3) == k, dk, wide)
        mean = [mean[g] + dk * Kf[g, 8 * k : 8 * k + 8, :] for g in range(3)]
    same = jnp.bitwise_and(jnp.right_shift(lane8, 1), 3) == jnp.right_shift(sub8, 1)
    for g in range(3):
        part = jnp.where(same, share[g : g + 1, :] * wide, 0.0)
        shift = jnp.broadcast_to(jnp.sum(part, axis=1, keepdims=True), (8, 256))
        M[8 * g : 8 * g + 8, :] = mean[g] - wet8 * shift
    for fl in range(12):
        c = pltpu.make_async_copy(M.at[pl.ds(2 * fl, 2), :], mrow_out.at[fl], out_sem.at[24 + fl])
        c.start()
        outs.append(c)
    for c in outs:
        c.wait()
    for c in sends:
        c.wait_send()


def local(ensemble, velocity, diffusivity, land_mask, obs_index, obs_owner, obs_value, obs_error):
    hbm = pl.BlockSpec(memory_space=pltpu.HBM)
    vm = lambda *shape, t=F32: pltpu.VMEM(shape, t)
    dma = lambda n: pltpu.SemaphoreType.DMA((n,))
    x1, mrow = pl.pallas_call(
        kernel,
        out_shape=(jax.ShapeDtypeStruct((80, 12, 2, 256), F32), jax.ShapeDtypeStruct((12, 2, 256), F32)),
        in_specs=[hbm] * 8,
        out_specs=(pl.BlockSpec(memory_space=pl.ANY), pl.BlockSpec(memory_space=pl.ANY)),
        scratch_shapes=[
            pltpu.SMEM((4,), F32), pltpu.SMEM((4, 4, 8), jnp.int32), pltpu.SMEM((4,), jnp.int32),
            pltpu.SMEM((4, 8), F32), pltpu.SMEM((4, 8), F32),
            vm(10, 12, 16, 256), vm(2, 3, 16, 256), vm(16, 256, t=jnp.int32), vm(10, 12, 16, 256),
            vm(20, 12, 8, 256), vm(2, 16, 128), vm(2, 2, 16, 128), vm(2, 16, 128), vm(2, 2, 8, 128),
            vm(16, 128), vm(15, 16, 128), vm(8, 16, 128), vm(32, 32, 128), vm(32, 8, 256),
            vm(32, 128), vm(32, 128), vm(32, 128), vm(32, 128), vm(32, 32, 128),
            vm(256, 640, t=BF16), vm(256, 640, t=BF16), vm(640, 256, t=BF16), vm(640, 256, t=BF16),
            vm(3, 256, 256), vm(3, 256, 256, t=BF16), vm(3, 256, 256, t=BF16),
            vm(2, 8, 256), vm(15, 8, 256), vm(7, 8, 256), vm(24, 256),
            dma(10), dma(7), dma(36), dma(2), dma(2), dma(7), dma(7), dma(42), dma(42),
            dma(15), dma(15), dma(7), dma(7), dma(15), dma(15), dma(7), dma(7),
        ],
        compiler_params=pltpu.CompilerParams(collective_id=0, has_side_effects=True, vmem_limit_bytes=58 << 20),
    )(
        ensemble.reshape(10, 12, 16, 256),
        velocity,
        land_mask,
        diffusivity,
        jnp.transpose(obs_index, (0, 2, 1)),
        obs_owner,
        obs_value,
        obs_error,
    )
    return (x1 + mrow[None]).reshape(80, 4, 3, 2, 256)


def solution(mesh):
    in_specs = (
        P("member", None, None, None, "domain"),
        P(None, None, None, "domain"),
        P(),
        P(None, "domain"),
        P(),
        P(),
        P(),
        P(),
    )
    out_specs = P(None, None, None, "member", "domain")
    return jax.shard_map(local, mesh=mesh, in_specs=in_specs, out_specs=out_specs, check_vma=False)
```

```python
import jax
import jax.numpy as jnp
from jax import lax
from jax.experimental import pallas as pl
from jax.experimental.pallas import tpu as pltpu
from jax.sharding import PartitionSpec as P

LOC_RADIUS = 64.0
MEM, DOM = 8, 16
FAR_FIRST = (5, 3, 7, 4, 1, 2, 6)
NEAR_LAST = (5, 13, 3, 7, 11, 15, 12, 4, 1, 9, 10, 14, 2, 6, 8)
MESH = pl.DeviceIdType.MESH
F32, BF16 = jnp.float32, jnp.bfloat16
HIGH = lax.Precision.HIGHEST


def gaspari(distance):
    scaled = distance * (1.0 / LOC_RADIUS)
    safe = jnp.maximum(scaled, 1.0)
    near = (((-0.25 * scaled + 0.5) * scaled + 0.625) * scaled - 5.0 / 3.0) * scaled * scaled + 1.0
    far = (
        ((((scaled * (1.0 / 12.0) - 0.5) * scaled + 0.625) * scaled + 5.0 / 3.0) * scaled - 5.0) * scaled
        + 4.0
        - (2.0 / 3.0) / safe
    )
    return jnp.where(scaled <= 1.0, near, jnp.where(scaled < 2.0, far, 0.0))


def separation(row_a, col_a, row_b, col_b):
    gap = jnp.abs(col_a - col_b)
    gap = jnp.minimum(gap, 4096 - gap)
    rows = row_a - row_b
    return jnp.sqrt((gap * gap + rows * rows).astype(F32))


def iota(shape, dim):
    return lax.broadcasted_iota(jnp.int32, shape, dim)


def halves(x):
    hi = x.astype(BF16)
    return hi, (x - hi.astype(F32)).astype(BF16)


def mm(a, b):
    return jnp.dot(a, b, preferred_element_type=F32)


def mm_nt(a, b, precision=None):
    return lax.dot_general(a, b, (((1,), (1,)), ((), ())), precision=precision, preferred_element_type=F32)


def kernel(
    ens, vel, mask, diff_in, oidx_in, oown_in, oval_in, oerr_in, x1_out, mrow_out,
    diff, oidx, oown, oval, oerr, E, V, W, F, D, pack, halo, corr, CR, vbuf, vtmp, vin, vin2, Z, RB, TP, Pm, Zi, bcol, gcol, LB,
    L1h, L1l, L2h, L2l, Kf, Kh, Kl, sbuf, sin1, sin2, M,
    in_sem, loc_sem, out_sem, hs, hr, cs, cr, as_, ar, d1s, d1r, m1s, m1r, d2s, d2r, m2s, m2r,
):
    me, dom = lax.axis_index("member"), lax.axis_index("domain")

    small = ((vel, V), (mask, W), (diff_in, diff), (oidx_in, oidx), (oown_in, oown), (oval_in, oval), (oerr_in, oerr))
    small = [pltpu.make_async_copy(src, dst, in_sem.at[3 + i]) for i, (src, dst) in enumerate(small)]
    copies = []
    for g in range(3):
        copies.append(pltpu.make_async_copy(ens.at[:, pl.ds(4 * g, 4)], E.at[:, pl.ds(4 * g, 4)], in_sem.at[g]))
    for c in small + copies:
        c.start()
    barrier = pltpu.get_barrier_semaphore()
    right, left = lax.rem(dom + 1, DOM), lax.rem(dom + DOM - 1, DOM)

    def across(i):
        return {"member": jnp.bitwise_xor(me, i % 8), "domain": jnp.bitwise_xor(dom, 8 * (i // 8))}

    def along(i):
        return {"domain": jnp.bitwise_xor(dom, i)}

    for where in [across(i) for i in range(1, 16)] + [along(i) for i in range(1, 8)]:
        pl.semaphore_signal(barrier, inc=1, device_id=where, device_id_type=MESH)
    for where in (left, right):
        pl.semaphore_signal(barrier, inc=1, device_id={"domain": where}, device_id_type=MESH)
    for c in small:
        c.wait()

    wet = W[...].astype(F32)
    row, col = iota((16, 256), 0), iota((16, 256), 1)
    lane16 = iota((16, 128), 1)
    even = jnp.bitwise_and(lane16, 1) == 0
    slot_fl = jnp.right_shift(lane16, 1)
    for _ in range(4):
        slot_fl = jnp.where(slot_fl >= 12, slot_fl - 12, slot_fl)
    slot_fl = jnp.where(lane16 < 120, slot_fl, -1)

    def interior(fl, acc):
        acc = list(acc)
        lev, fld = lax.rem(fl, 3), lax.div(fl, 3)
        u, v, d = V[0, lev], V[1, lev], diff[fld]
        cen = wet * (1.0 - 4.0 * d)
        east, west = wet * (d - 0.5 * u), wet * (d + 0.5 * u)
        north, south = wet * (d - 0.5 * v), wet * (d + 0.5 * v)
        ours = slot_fl == fl
        acc[2] = jnp.where(ours & even, jnp.broadcast_to(east[:, 255:256], (16, 128)), acc[2])
        acc[2] = jnp.where(ours & ~even, jnp.broadcast_to(west[:, 0:1], (16, 128)), acc[2])
        east, west = jnp.where(col == 255, 0.0, east), jnp.where(col == 0, 0.0, west)
        north, south = jnp.where(row == 15, 0.0, north), jnp.where(row == 0, 0.0, south)
        for m in range(10):
            x = E[m, fl]
            F[m, fl] = (
                cen * x
                + east * pltpu.roll(x, 255, 1)
                + west * pltpu.roll(x, 1, 1)
                + north * pltpu.roll(x, 15, 0)
                + south * pltpu.roll(x, 1, 0)
            )
            slot = 2 * ((m % 5) * 12 + fl)
            edges = pltpu.roll(jnp.where(lane16 == 0, x[:, :128], x[:, 128:]), slot, 1)
            here = (lane16 == slot) | (lane16 == jnp.bitwise_and(slot + 127, 127))
            acc[m // 5] = jnp.where(here, edges, acc[m // 5])
        return tuple(acc)

    acc = tuple(jnp.zeros((16, 128), F32) for _ in range(3))
    copies[0].wait()
    acc = lax.fori_loop(0, 4, interior, acc)

    pl.semaphore_wait(barrier, 24)
    sends = []

    def remote(src, dst, send, recv, where):
        c = pltpu.make_async_remote_copy(
            src_ref=src, dst_ref=dst, send_sem=send, recv_sem=recv, device_id=where, device_id_type=MESH
        )
        c.start()
        sends.append(c)
        return c

    arrivals, locals_ = [], []
    own_rows, own_slot = pl.ds(2 * me, 2), pl.ds(2 * lax.rem(me, 4), 2)
    half = lax.div(me, 4)

    def scatter(g):
        fls = pl.ds(g, 1)
        mine = D.at[pl.ds(10 * half, 10), fls, own_slot, :]
        c = pltpu.make_async_copy(F.at[:, fls, own_rows, :], mine, loc_sem.at[g])
        c.start()
        locals_.append(c)
        for i in FAR_FIRST:
            t = jnp.bitwise_xor(me, i)
            n = 7 * g + i - 1
            arrivals.append(remote(F.at[:, fls, pl.ds(2 * t, 2), :], mine, as_.at[n], ar.at[n], {"member": t}))

    scatter(0)
    scatter(1)
    for g in (1, 2):
        copies[g].wait()
        acc = lax.fori_loop(4 * g, 4 * g + 4, interior, acc)
    pack[0], pack[1] = acc[0], acc[1]

    to_left = remote(pack, halo.at[0], hs.at[0], hr.at[0], {"domain": left})
    to_right = remote(pack, halo.at[1], hs.at[1], hr.at[1], {"domain": right})

    lane32, sub32 = iota((32, 128), 1), iota((32, 128), 0)

    def wide_l(x, rows):
        return jnp.broadcast_to(x[0:1, :], (rows, 128))

    zi = jnp.zeros((32, 128), jnp.int32)
    row_s, col_s, fl_s, row_l, col_l, fl_l = zi, zi, zi, zi, zi, zi
    val_s = jnp.zeros((32, 128), F32)
    places = []
    for k in range(32):
        b, n = k // 8, k % 8
        own = oown[b]
        r = jnp.right_shift(own, 4) * 2 + oidx[b, 2, n]
        c = jnp.bitwise_and(own, 15) * 256 + oidx[b, 3, n]
        f = oidx[b, 0, n] * 3 + oidx[b, 1, n]
        places.append((r, c))
        row_s, col_s, fl_s = (jnp.where(sub32 == k, s, a) for s, a in ((r, row_s), (c, col_s), (f, fl_s)))
        row_l, col_l, fl_l = (jnp.where(lane32 == k, s, a) for s, a in ((r, row_l), (c, col_l), (f, fl_l)))
        val_s = jnp.where(sub32 == k, oval[b, n], val_s)
    pick = (iota((256, 128), 0) + dom * 256 == wide_l(col_l, 256)) & (iota((256, 128), 1) < 32)
    pick = jnp.where(pick, 1.0, 0.0).astype(BF16)
    at_row = jnp.bitwise_and(iota((160, 128), 0), 15) == wide_l(row_l, 160)
    got = jnp.zeros((160, 128), F32)
    for fl in range(12):
        x = F[:, fl].reshape(160, 256)
        hi = x.astype(BF16)
        rest = x - hi.astype(F32)
        mid, lo = halves(rest)
        got = jnp.where(wide_l(fl_l, 160) == fl, mm(hi, pick) + (mm(mid, pick) + mm(lo, pick)), got)
    got = jnp.where(at_row, got, 0.0)
    seen = jnp.sum(got.reshape(10, 16, 128), axis=1)
    tile_l, edge_l = jnp.right_shift(col_l, 8), jnp.bitwise_and(col_l, 255)
    some = lane32 < 32
    at_last, at_first = some & (edge_l == 255), some & (edge_l == 0)
    spot = jnp.where(at_first & (jnp.bitwise_and(tile_l + 15, 15) == dom), 2 * fl_l - 1, -1000)
    spot = jnp.where(at_last & (jnp.bitwise_and(tile_l + 1, 15) == dom), 2 * fl_l, spot)
    coef = jnp.where(at_first & (tile_l == dom), 2 * fl_l + 1, jnp.where(at_last & (tile_l == dom), 2 * fl_l, -1000))
    spot, coef = wide_l(pltpu.roll(spot, 32, 1), 128), wide_l(pltpu.roll(coef, 64, 1), 128)
    picks = [spot + 24 * u for u in range(5)]
    picks = [jnp.where(p == -1, 127, p) for p in picks] + [coef]
    picks = jnp.concatenate([jnp.where(iota((128, 128), 0) == p, 1.0, 0.0).astype(BF16) for p in picks], axis=1)
    rest = jnp.concatenate([acc[0], acc[1], acc[2]], axis=0)
    hi = rest.astype(BF16)
    mid, lo = halves(rest - hi.astype(F32))
    extra = mm(hi, picks) + (mm(mid, picks) + mm(lo, picks))
    in_row = iota((16, 128), 0) == wide_l(pltpu.roll(row_l, 32, 1), 16)
    in_row2 = iota((16, 128), 0) == wide_l(pltpu.roll(row_l, 64, 1), 16)
    vtmp[...] = jnp.zeros((16, 128), F32)
    for m in range(10):
        part = extra[16 * (m // 5) : 16 * (m // 5) + 16, 128 * (m % 5) : 128 * (m % 5) + 128]
        vtmp[m : m + 1, :] = seen[m : m + 1, :] + jnp.sum(jnp.where(in_row, part, 0.0), axis=0, keepdims=True)
    part = jnp.sum(jnp.where(in_row2, extra[32:48, 640:768], 0.0), axis=0, keepdims=True)
    high = pltpu.roll(vtmp[8:16, :], 64, 1)
    vbuf[...] = vtmp[0:8, :] + jnp.where(iota((8, 128), 0) == 2, part, high)
    parts_a = [
        remote(vbuf, vin.at[i], d1s.at[i - 1], d1r.at[i - 1], across(i)) for i in NEAR_LAST
    ]
    for g in range(2, 4):
        scatter(g)

    to_left.wait_recv()
    to_right.wait_recv()
    for h in range(2):
        corr[h] = jnp.where(even, halo[0, h], pltpu.roll(halo[1, h], 2, 1)) * acc[2]
    fixes = []
    mine = CR.at[half, :, own_slot, :]
    own_corr = pltpu.make_async_copy(corr.at[:, own_rows, :], mine, loc_sem.at[12])
    own_corr.start()
    for i in FAR_FIRST:
        t = jnp.bitwise_xor(me, i)
        fixes.append(remote(corr.at[:, pl.ds(2 * t, 2), :], mine, cs.at[i - 1], cr.at[i - 1], {"member": t}))
    for g in range(4, 12):
        scatter(g)

    rho = gaspari(separation(row_s, col_s, row_l, col_l))
    for k in range(32):
        RB[k] = jnp.broadcast_to(rho[:, k : k + 1], (32, 128))


    sub8, lane8 = iota((8, 256), 0), iota((8, 256), 1)
    odd = jnp.bitwise_and(sub8, 1) == 1
    wet0 = jnp.broadcast_to(W[pl.ds(2 * me, 1), :].astype(F32), (8, 256))
    wet1 = jnp.broadcast_to(W[pl.ds(2 * me + 1, 1), :].astype(F32), (8, 256))
    wet8 = jnp.where(odd, wet1, wet0)
    row8, col8 = 2 * me + jnp.bitwise_and(sub8, 1), dom * 256 + lane8
    for k in range(32):
        TP[k] = gaspari(separation(row8, col8, places[k][0], places[k][1])) * wet8

    for c in parts_a:
        c.wait_recv()
    vin[0] = vbuf[...]
    for i in range(8):
        Z[jnp.bitwise_xor(me, i)] = vin[i] + vin[i + 8]
    parts_b = [remote(Z, vin2.at[i - 1], m1s.at[i - 1], m1r.at[i - 1], along(i)) for i in (4, 5, 2, 3, 6, 7, 1)]
    for c in parts_b:
        c.wait_recv()
    total = Z[...]
    for i in range(7):
        total = total + vin2[i]
    total = jnp.concatenate([total, pltpu.roll(total, 64, 2)], axis=1)

    Y = jnp.transpose(total.reshape(128, 128))
    real = jnp.bitwise_and(lane32, 15) < 10
    Y = jnp.where(real, Y[0:32] + Y[32:64] * jnp.broadcast_to(Y[0:32, 10:11], (32, 128)), 0.0)
    ybar = jnp.broadcast_to(jnp.sum(Y, axis=1, keepdims=True) * (1.0 / 80.0), (32, 128))
    A = jnp.where(real, Y - ybar, 0.0)
    inv = jnp.where(lane32 == sub32, 1.0, 0.0).astype(F32)
    for k in range(32):
        a, z = A[k : k + 1, :], inv[k : k + 1, :]
        cov = jnp.broadcast_to(jnp.sum(A * a, axis=1, keepdims=True), (32, 128))
        err = oerr[k // 8, k % 8]
        den = cov[k : k + 1, :] * (1.0 / 79.0) + err
        gain = 1.0 / (79.0 * den)
        beta = 1.0 / (1.0 + jnp.sqrt(err / den))
        Pm[k : k + 1, :] = a
        Zi[k : k + 1, :] = z
        bcol[k : k + 1, :] = beta
        gcol[k : k + 1, :] = gain
        step = RB[k] * cov * gain
        A = A - (step * beta) * a
        inv = inv - step * z

    Pv = Pm[...]
    Pb = Pv * bcol[...]
    low = mm_nt(Pv, Pb, HIGH)
    for j in range(31):
        LB[j] = jnp.broadcast_to(low[:, j : j + 1], (32, 128))
    for k in range(32):
        TP[k] = TP[k] * jnp.broadcast_to(gcol[k : k + 1, 0:1], (8, 256))

    n = iota((128, 640), 1)
    unit = jnp.right_shift(n, 5)
    q = jnp.bitwise_and(jnp.right_shift(n, 1), 3)
    upper = (unit >= 10).astype(jnp.int32)
    spread = jnp.where((4 * upper + q) * 16 + unit - 10 * upper == iota((128, 640), 0), 1.0, 0.0).astype(BF16)
    n = iota((8, 640), 1)
    match = jnp.bitwise_and(jnp.right_shift(n, 3), 3) * 2 + jnp.bitwise_and(n, 1) == iota((8, 640), 0)
    keep = jnp.broadcast_to(jnp.where(match, 1.0, 0.0)[None], (32, 8, 640))

    def kron(part):
        return (jnp.broadcast_to(mm(part, spread)[:, None, :], (32, 8, 640)) * keep).reshape(256, 640)

    hi, lo = halves(Pv)
    L1h[...] = kron(hi).astype(BF16)
    L1l[...] = kron(lo).astype(BF16)
    hi, lo = halves(Pb)
    L2h[...] = jnp.transpose(kron(hi)).astype(BF16)
    L2l[...] = jnp.transpose(kron(lo)).astype(BF16)
    invT = jnp.transpose(jnp.concatenate([Zi[...], jnp.zeros((96, 128), F32)], axis=0))[:32]

    sums = jnp.zeros((8, 256), F32)
    own_corr.wait()
    for c in fixes:
        c.wait_recv()
    first, last = iota((8, 128), 1) == 0, iota((8, 128), 1) == 127

    def amend(fl, carry):
        for u in range(20):
            y = pltpu.roll(CR[u // 10, u % 10 // 5], 127 - 2 * ((u % 5) * 12 + fl), 1)
            D[u, fl, :, 0:128] = D[u, fl, :, 0:128] + jnp.where(first, y, 0.0)
            D[u, fl, :, 128:256] = D[u, fl, :, 128:256] + jnp.where(last, y, 0.0)
        return carry

    for g in range(3):
        for u in range(4 * g, 4 * g + 4):
            locals_[u].wait()
            for c in arrivals[7 * u : 7 * u + 7]:
                c.wait_recv()
        lax.fori_loop(4 * g, 4 * g + 4, amend, 0)
        xh, xl = halves(D[:, 4 * g : 4 * g + 4].reshape(640, 256))
        cov = mm(L1h[...], xh) + (mm(L1h[...], xl) + mm(L1l[...], xh))
        gains = []
        for k in range(32):
            left_, right_ = cov[8 * k : 8 * k + 8, :128], cov[8 * k : 8 * k + 8, 128:]
            for j in range(k):
                s = jnp.broadcast_to(LB[j, k : k + 1, :], (8, 128))
                left_, right_ = left_ - s * gains[j][0], right_ - s * gains[j][1]
            left_, right_ = left_ * TP[k, :, 0:128], right_ * TP[k, :, 128:256]
            gains.append((left_, right_))
            Kf[g, 8 * k : 8 * k + 8, 0:128] = left_
            Kf[g, 8 * k : 8 * k + 8, 128:256] = right_
        hi, lo = halves(Kf[g])
        Kh[g], Kl[g] = hi, lo
        pick = jnp.where(sub8 == g, 1.0, 0.0).astype(BF16)
        sums = sums + (mm_nt(pick, hi) + mm_nt(pick, lo))
    sbuf[0] = jnp.where(sub8 == 3, wet0 + wet1, sums)
    parts = [
        remote(sbuf.at[0], sin2.at[i - 1], m2s.at[i - 1], m2r.at[i - 1], along(i)) for i in (4, 5, 2, 3, 6, 7, 1)
    ]

    outs = []

    def update(g):
        change = mm(L2h[...], Kh[g]) + (mm(L2h[...], Kl[g]) + mm(L2l[...], Kh[g]))
        D[:, 4 * g : 4 * g + 4] = D[:, 4 * g : 4 * g + 4] - change.reshape(20, 4, 8, 256)
        for s in range(8):
            c = pltpu.make_async_copy(
                D.at[pl.ds(10 * (s // 4), 10), pl.ds(4 * g, 4), pl.ds(2 * (s % 4), 2), :],
                x1_out.at[pl.ds(10 * s, 10), pl.ds(4 * g, 4), :, :],
                out_sem.at[8 * g + s],
            )
            c.start()
            outs.append(c)

    update(0)
    update(1)
    total = sbuf[0]
    for c in parts:
        c.wait_recv()
    for i in range(7):
        total = total + sin2[i]
    sbuf[1] = total
    parts = [
        remote(sbuf.at[1], sin1.at[i - 1], d2s.at[i - 1], d2r.at[i - 1], across(i)) for i in NEAR_LAST
    ]
    update(2)
    for c in parts:
        c.wait_recv()
    for i in range(15):
        total = total + sin1[i]

    cells = jnp.sum(jnp.sum(jnp.where(sub8 == 3, total, 0.0), axis=1, keepdims=True), axis=0, keepdims=True)
    share = total * (1.0 / jnp.broadcast_to(cells, (8, 256)))
    fl_w = jnp.concatenate([fl_s, fl_s], axis=1)
    picked = jnp.zeros((32, 256), F32)
    for g in range(3):
        picked = jnp.where(jnp.right_shift(fl_w, 2) == g, share[g : g + 1, :], picked)
    four = jnp.bitwise_and(jnp.right_shift(iota((32, 256), 1), 1), 3)
    picked = jnp.where(four == jnp.bitwise_and(fl_w, 3), picked, 0.0)
    fold = jnp.where(jnp.right_shift(iota((256, 128), 0), 3) == iota((256, 128), 1), 1.0, 0.0).astype(BF16)
    hi, lo = halves(picked)
    shifts = mm(hi, fold) + mm(lo, fold)
    shifts = jnp.where(jnp.right_shift(lane32, 3) < jnp.right_shift(sub32, 3), shifts, 0.0)
    base = val_s - ybar
    innov = jnp.sum(invT * base, axis=0, keepdims=True)
    for _ in range(3):
        moved = base + jnp.sum(shifts * innov, axis=1, keepdims=True)
        innov = jnp.sum(invT * moved, axis=0, keepdims=True)
    wide = jnp.zeros((8, 256), F32)
    mean = [jnp.zeros((8, 256), F32) for _ in range(3)]
    for k in range(32):
        dk = jnp.broadcast_to(innov[0:1, k : k + 1], (8, 256))
        wide = jnp.where(jnp.right_shift(lane8, 3) == k, dk, wide)
        mean = [mean[g] + dk * Kf[g, 8 * k : 8 * k + 8, :] for g in range(3)]
    same = jnp.bitwise_and(jnp.right_shift(lane8, 1), 3) == jnp.right_shift(sub8, 1)
    for g in range(3):
        part = jnp.where(same, share[g : g + 1, :] * wide, 0.0)
        shift = jnp.broadcast_to(jnp.sum(part, axis=1, keepdims=True), (8, 256))
        M[8 * g : 8 * g + 8, :] = mean[g] - wet8 * shift
    for fl in range(12):
        c = pltpu.make_async_copy(M.at[pl.ds(2 * fl, 2), :], mrow_out.at[fl], out_sem.at[24 + fl])
        c.start()
        outs.append(c)
    for c in outs:
        c.wait()
    for c in sends:
        c.wait_send()


def local(ensemble, velocity, diffusivity, land_mask, obs_index, obs_owner, obs_value, obs_error):
    hbm = pl.BlockSpec(memory_space=pltpu.HBM)
    vm = lambda *shape, t=F32: pltpu.VMEM(shape, t)
    dma = lambda n: pltpu.SemaphoreType.DMA((n,))
    x1, mrow = pl.pallas_call(
        kernel,
        out_shape=(jax.ShapeDtypeStruct((80, 12, 2, 256), F32), jax.ShapeDtypeStruct((12, 2, 256), F32)),
        in_specs=[hbm] * 8,
        out_specs=(pl.BlockSpec(memory_space=pl.ANY), pl.BlockSpec(memory_space=pl.ANY)),
        scratch_shapes=[
            pltpu.SMEM((4,), F32), pltpu.SMEM((4, 4, 8), jnp.int32), pltpu.SMEM((4,), jnp.int32),
            pltpu.SMEM((4, 8), F32), pltpu.SMEM((4, 8), F32),
            vm(10, 12, 16, 256), vm(2, 3, 16, 256), vm(16, 256, t=jnp.int32), vm(10, 12, 16, 256),
            vm(20, 12, 8, 256), vm(2, 16, 128), vm(2, 2, 16, 128), vm(2, 16, 128), vm(2, 2, 8, 128),
            vm(8, 128), vm(16, 128), vm(16, 8, 128), vm(7, 8, 8, 128), vm(8, 8, 128), vm(32, 32, 128), vm(32, 8, 256),
            vm(32, 128), vm(32, 128), vm(32, 128), vm(32, 128), vm(32, 32, 128),
            vm(256, 640, t=BF16), vm(256, 640, t=BF16), vm(640, 256, t=BF16), vm(640, 256, t=BF16),
            vm(3, 256, 256), vm(3, 256, 256, t=BF16), vm(3, 256, 256, t=BF16),
            vm(2, 8, 256), vm(15, 8, 256), vm(7, 8, 256), vm(24, 256),
            dma(10), dma(13), dma(36), dma(2), dma(2), dma(7), dma(7), dma(84), dma(84),
            dma(15), dma(15), dma(7), dma(7), dma(15), dma(15), dma(7), dma(7),
        ],
        compiler_params=pltpu.CompilerParams(collective_id=0, has_side_effects=True, vmem_limit_bytes=58 << 20),
    )(
        ensemble.reshape(10, 12, 16, 256),
        velocity,
        land_mask,
        diffusivity,
        jnp.transpose(obs_index, (0, 2, 1)),
        obs_owner,
        obs_value,
        obs_error,
    )
    return (x1 + mrow[None]).reshape(80, 4, 3, 2, 256)


def solution(mesh):
    in_specs = (
        P("member", None, None, None, "domain"),
        P(None, None, None, "domain"),
        P(),
        P(None, "domain"),
        P(),
        P(),
        P(),
        P(),
    )
    out_specs = P(None, None, None, "member", "domain")
    return jax.shard_map(local, mesh=mesh, in_specs=in_specs, out_specs=out_specs, check_vma=False)
```

```python
import jax
import jax.numpy as jnp
from jax import lax
from jax.experimental import pallas as pl
from jax.experimental.pallas import tpu as pltpu
from jax.sharding import PartitionSpec as P

LOC_RADIUS = 64.0
MEM, DOM = 8, 16
FAR_FIRST = (5, 3, 7, 4, 1, 2, 6)
NEAR_LAST = (5, 13, 3, 7, 11, 15, 12, 4, 1, 9, 10, 14, 2, 6, 8)
MESH = pl.DeviceIdType.MESH
F32, BF16 = jnp.float32, jnp.bfloat16
HIGH = lax.Precision.HIGHEST


def gaspari(distance):
    scaled = distance * (1.0 / LOC_RADIUS)
    safe = jnp.maximum(scaled, 1.0)
    near = (((-0.25 * scaled + 0.5) * scaled + 0.625) * scaled - 5.0 / 3.0) * scaled * scaled + 1.0
    far = (
        ((((scaled * (1.0 / 12.0) - 0.5) * scaled + 0.625) * scaled + 5.0 / 3.0) * scaled - 5.0) * scaled
        + 4.0
        - (2.0 / 3.0) / safe
    )
    return jnp.where(scaled <= 1.0, near, jnp.where(scaled < 2.0, far, 0.0))


def separation(row_a, col_a, row_b, col_b):
    gap = jnp.abs(col_a - col_b)
    gap = jnp.minimum(gap, 4096 - gap)
    rows = row_a - row_b
    return jnp.sqrt((gap * gap + rows * rows).astype(F32))


def iota(shape, dim):
    return lax.broadcasted_iota(jnp.int32, shape, dim)


def halves(x):
    hi = x.astype(BF16)
    return hi, (x - hi.astype(F32)).astype(BF16)


def mm(a, b):
    return jnp.dot(a, b, preferred_element_type=F32)


def mm_nt(a, b, precision=None):
    return lax.dot_general(a, b, (((1,), (1,)), ((), ())), precision=precision, preferred_element_type=F32)


def kernel(
    ens, vel, mask, diff_in, oidx_in, oown_in, oval_in, oerr_in, x1_out, mrow_out,
    diff, oidx, oown, oval, oerr, E, V, W, F, D, pack, halo, corr, CR, vbuf, vtmp, vin, vin2, Z, RB, TP, Pm, Zi, bcol, gcol, LB,
    L1h, L1l, L2h, L2l, Kf, Kh, Kl, sbuf, sin1, sin2, M, TQ, Kd,
    in_sem, loc_sem, out_sem, hs, hr, cs, cr, as_, ar, d1s, d1r, m1s, m1r, d2s, d2r, m2s, m2r,
):
    me, dom = lax.axis_index("member"), lax.axis_index("domain")

    small = ((vel, V), (mask, W), (diff_in, diff), (oidx_in, oidx), (oown_in, oown), (oval_in, oval), (oerr_in, oerr))
    small = [pltpu.make_async_copy(src, dst, in_sem.at[3 + i]) for i, (src, dst) in enumerate(small)]
    copies = []
    for g in range(3):
        copies.append(pltpu.make_async_copy(ens.at[:, pl.ds(4 * g, 4)], E.at[:, pl.ds(4 * g, 4)], in_sem.at[g]))
    for c in small + copies:
        c.start()
    barrier = pltpu.get_barrier_semaphore()
    right, left = lax.rem(dom + 1, DOM), lax.rem(dom + DOM - 1, DOM)

    def across(i):
        return {"member": jnp.bitwise_xor(me, i % 8), "domain": jnp.bitwise_xor(dom, 8 * (i // 8))}

    def along(i):
        return {"domain": jnp.bitwise_xor(dom, i)}

    for where in [across(i) for i in range(1, 16)] + [along(i) for i in range(1, 8)]:
        pl.semaphore_signal(barrier, inc=1, device_id=where, device_id_type=MESH)
    for where in (left, right):
        pl.semaphore_signal(barrier, inc=1, device_id={"domain": where}, device_id_type=MESH)
    for c in small:
        c.wait()

    wet = W[...].astype(F32)
    row, col = iota((16, 256), 0), iota((16, 256), 1)
    lane16 = iota((16, 128), 1)
    even = jnp.bitwise_and(lane16, 1) == 0
    slot_fl = jnp.right_shift(lane16, 1)
    for _ in range(4):
        slot_fl = jnp.where(slot_fl >= 12, slot_fl - 12, slot_fl)
    slot_fl = jnp.where(lane16 < 120, slot_fl, -1)

    def interior(fl, acc):
        acc = list(acc)
        lev, fld = lax.rem(fl, 3), lax.div(fl, 3)
        u, v, d = V[0, lev], V[1, lev], diff[fld]
        cen = wet * (1.0 - 4.0 * d)
        east, west = wet * (d - 0.5 * u), wet * (d + 0.5 * u)
        north, south = wet * (d - 0.5 * v), wet * (d + 0.5 * v)
        ours = slot_fl == fl
        acc[2] = jnp.where(ours & even, jnp.broadcast_to(east[:, 255:256], (16, 128)), acc[2])
        acc[2] = jnp.where(ours & ~even, jnp.broadcast_to(west[:, 0:1], (16, 128)), acc[2])
        east, west = jnp.where(col == 255, 0.0, east), jnp.where(col == 0, 0.0, west)
        north, south = jnp.where(row == 15, 0.0, north), jnp.where(row == 0, 0.0, south)
        for m in range(10):
            x = E[m, fl]
            F[m, fl] = (
                cen * x
                + east * pltpu.roll(x, 255, 1)
                + west * pltpu.roll(x, 1, 1)
                + north * pltpu.roll(x, 15, 0)
                + south * pltpu.roll(x, 1, 0)
            )
            slot = 2 * ((m % 5) * 12 + fl)
            edges = pltpu.roll(jnp.where(lane16 == 0, x[:, :128], x[:, 128:]), slot, 1)
            here = (lane16 == slot) | (lane16 == jnp.bitwise_and(slot + 127, 127))
            acc[m // 5] = jnp.where(here, edges, acc[m // 5])
        return tuple(acc)

    acc = tuple(jnp.zeros((16, 128), F32) for _ in range(3))
    copies[0].wait()
    acc = lax.fori_loop(0, 4, interior, acc)

    pl.semaphore_wait(barrier, 24)
    sends = []

    def remote(src, dst, send, recv, where):
        c = pltpu.make_async_remote_copy(
            src_ref=src, dst_ref=dst, send_sem=send, recv_sem=recv, device_id=where, device_id_type=MESH
        )
        c.start()
        sends.append(c)
        return c

    arrivals, locals_ = [], []
    own_rows, own_slot = pl.ds(2 * me, 2), pl.ds(2 * lax.rem(me, 4), 2)
    half = lax.div(me, 4)

    def scatter(g):
        fls = pl.ds(g, 1)
        mine = D.at[pl.ds(10 * half, 10), fls, own_slot, :]
        c = pltpu.make_async_copy(F.at[:, fls, own_rows, :], mine, loc_sem.at[g])
        c.start()
        locals_.append(c)
        for i in FAR_FIRST:
            t = jnp.bitwise_xor(me, i)
            n = 7 * g + i - 1
            arrivals.append(remote(F.at[:, fls, pl.ds(2 * t, 2), :], mine, as_.at[n], ar.at[n], {"member": t}))

    scatter(0)
    scatter(1)
    for g in (1, 2):
        copies[g].wait()
        acc = lax.fori_loop(4 * g, 4 * g + 4, interior, acc)
    pack[0], pack[1] = acc[0], acc[1]

    to_left = remote(pack, halo.at[0], hs.at[0], hr.at[0], {"domain": left})
    to_right = remote(pack, halo.at[1], hs.at[1], hr.at[1], {"domain": right})

    lane32, sub32 = iota((32, 128), 1), iota((32, 128), 0)

    def wide_l(x, rows):
        return jnp.broadcast_to(x[0:1, :], (rows, 128))

    zi = jnp.zeros((32, 128), jnp.int32)
    row_s, col_s, fl_s, row_l, col_l, fl_l = zi, zi, zi, zi, zi, zi
    val_s = jnp.zeros((32, 128), F32)
    places = []
    for k in range(32):
        b, n = k // 8, k % 8
        own = oown[b]
        r = jnp.right_shift(own, 4) * 2 + oidx[b, 2, n]
        c = jnp.bitwise_and(own, 15) * 256 + oidx[b, 3, n]
        f = oidx[b, 0, n] * 3 + oidx[b, 1, n]
        places.append((r, c))
        row_s, col_s, fl_s = (jnp.where(sub32 == k, s, a) for s, a in ((r, row_s), (c, col_s), (f, fl_s)))
        row_l, col_l, fl_l = (jnp.where(lane32 == k, s, a) for s, a in ((r, row_l), (c, col_l), (f, fl_l)))
        val_s = jnp.where(sub32 == k, oval[b, n], val_s)
    pick = (iota((256, 128), 0) + dom * 256 == wide_l(col_l, 256)) & (iota((256, 128), 1) < 32)
    pick = jnp.where(pick, 1.0, 0.0).astype(BF16)
    at_row = jnp.bitwise_and(iota((160, 128), 0), 15) == wide_l(row_l, 160)
    got = jnp.zeros((160, 128), F32)
    for fl in range(12):
        x = F[:, fl].reshape(160, 256)
        hi = x.astype(BF16)
        rest = x - hi.astype(F32)
        mid, lo = halves(rest)
        got = jnp.where(wide_l(fl_l, 160) == fl, mm(hi, pick) + (mm(mid, pick) + mm(lo, pick)), got)
    got = jnp.where(at_row, got, 0.0)
    seen = jnp.sum(got.reshape(10, 16, 128), axis=1)
    tile_l, edge_l = jnp.right_shift(col_l, 8), jnp.bitwise_and(col_l, 255)
    some = lane32 < 32
    at_last, at_first = some & (edge_l == 255), some & (edge_l == 0)
    spot = jnp.where(at_first & (jnp.bitwise_and(tile_l + 15, 15) == dom), 2 * fl_l - 1, -1000)
    spot = jnp.where(at_last & (jnp.bitwise_and(tile_l + 1, 15) == dom), 2 * fl_l, spot)
    coef = jnp.where(at_first & (tile_l == dom), 2 * fl_l + 1, jnp.where(at_last & (tile_l == dom), 2 * fl_l, -1000))
    spot, coef = wide_l(pltpu.roll(spot, 32, 1), 128), wide_l(pltpu.roll(coef, 64, 1), 128)
    picks = [spot + 24 * u for u in range(5)]
    picks = [jnp.where(p == -1, 127, p) for p in picks] + [coef]
    picks = jnp.concatenate([jnp.where(iota((128, 128), 0) == p, 1.0, 0.0).astype(BF16) for p in picks], axis=1)
    rest = jnp.concatenate([acc[0], acc[1], acc[2]], axis=0)
    hi = rest.astype(BF16)
    mid, lo = halves(rest - hi.astype(F32))
    extra = mm(hi, picks) + (mm(mid, picks) + mm(lo, picks))
    in_row = iota((16, 128), 0) == wide_l(pltpu.roll(row_l, 32, 1), 16)
    in_row2 = iota((16, 128), 0) == wide_l(pltpu.roll(row_l, 64, 1), 16)
    vtmp[...] = jnp.zeros((16, 128), F32)
    for m in range(10):
        part = extra[16 * (m // 5) : 16 * (m // 5) + 16, 128 * (m % 5) : 128 * (m % 5) + 128]
        vtmp[m : m + 1, :] = seen[m : m + 1, :] + jnp.sum(jnp.where(in_row, part, 0.0), axis=0, keepdims=True)
    part = jnp.sum(jnp.where(in_row2, extra[32:48, 640:768], 0.0), axis=0, keepdims=True)
    high = pltpu.roll(vtmp[8:16, :], 64, 1)
    vbuf[...] = vtmp[0:8, :] + jnp.where(iota((8, 128), 0) == 2, part, high)
    parts_a = [
        remote(vbuf, vin.at[i], d1s.at[i - 1], d1r.at[i - 1], across(i)) for i in NEAR_LAST
    ]
    for g in range(2, 4):
        scatter(g)

    to_left.wait_recv()
    to_right.wait_recv()
    for h in range(2):
        corr[h] = jnp.where(even, halo[0, h], pltpu.roll(halo[1, h], 2, 1)) * acc[2]
    fixes = []
    mine = CR.at[half, :, own_slot, :]
    own_corr = pltpu.make_async_copy(corr.at[:, own_rows, :], mine, loc_sem.at[12])
    own_corr.start()
    for i in FAR_FIRST:
        t = jnp.bitwise_xor(me, i)
        fixes.append(remote(corr.at[:, pl.ds(2 * t, 2), :], mine, cs.at[i - 1], cr.at[i - 1], {"member": t}))
    for g in range(4, 12):
        scatter(g)

    rho = gaspari(separation(row_s, col_s, row_l, col_l))
    for k in range(32):
        RB[k] = jnp.broadcast_to(rho[:, k : k + 1], (32, 128))


    sub8, lane8 = iota((8, 256), 0), iota((8, 256), 1)
    odd = jnp.bitwise_and(sub8, 1) == 1
    wet0 = jnp.broadcast_to(W[pl.ds(2 * me, 1), :].astype(F32), (8, 256))
    wet1 = jnp.broadcast_to(W[pl.ds(2 * me + 1, 1), :].astype(F32), (8, 256))
    wet8 = jnp.where(odd, wet1, wet0)
    row8, col8 = 2 * me + jnp.bitwise_and(sub8, 1), dom * 256 + lane8
    for k in range(32):
        TP[k] = gaspari(separation(row8, col8, places[k][0], places[k][1])) * wet8
        for h in range(2):
            taper = gaspari(separation(8 * h + sub8, col8, places[k][0], places[k][1]))
            TQ[32 * h + k] = taper * W[8 * h : 8 * h + 8, :].astype(F32)

    for c in parts_a:
        c.wait_recv()
    vin[0] = vbuf[...]
    for i in range(8):
        Z[jnp.bitwise_xor(me, i)] = vin[i] + vin[i + 8]
    parts_b = [remote(Z, vin2.at[i - 1], m1s.at[i - 1], m1r.at[i - 1], along(i)) for i in (4, 5, 2, 3, 6, 7, 1)]
    for c in parts_b:
        c.wait_recv()
    total = Z[...]
    for i in range(7):
        total = total + vin2[i]
    total = jnp.concatenate([total, pltpu.roll(total, 64, 2)], axis=1)

    Y = jnp.transpose(total.reshape(128, 128))
    real = jnp.bitwise_and(lane32, 15) < 10
    Y = jnp.where(real, Y[0:32] + Y[32:64] * jnp.broadcast_to(Y[0:32, 10:11], (32, 128)), 0.0)
    ybar = jnp.broadcast_to(jnp.sum(Y, axis=1, keepdims=True) * (1.0 / 80.0), (32, 128))
    A = jnp.where(real, Y - ybar, 0.0)
    inv = jnp.where(lane32 == sub32, 1.0, 0.0).astype(F32)
    for k in range(32):
        a, z = A[k : k + 1, :], inv[k : k + 1, :]
        cov = jnp.broadcast_to(jnp.sum(A * a, axis=1, keepdims=True), (32, 128))
        err = oerr[k // 8, k % 8]
        den = cov[k : k + 1, :] * (1.0 / 79.0) + err
        gain = 1.0 / (79.0 * den)
        beta = 1.0 / (1.0 + jnp.sqrt(err / den))
        Pm[k : k + 1, :] = a
        Zi[k : k + 1, :] = z
        bcol[k : k + 1, :] = beta
        gcol[k : k + 1, :] = gain
        step = RB[k] * cov * gain
        A = A - (step * beta) * a
        inv = inv - step * z

    Pv = Pm[...]
    Pb = Pv * bcol[...]
    low = mm_nt(Pv, Pb, HIGH)
    for j in range(31):
        LB[j] = jnp.broadcast_to(low[:, j : j + 1], (32, 128))
    for k in range(32):
        g_k = jnp.broadcast_to(gcol[k : k + 1, 0:1], (8, 256))
        TP[k] = TP[k] * g_k
        TQ[k] = TQ[k] * g_k
        TQ[32 + k] = TQ[32 + k] * g_k

    n = iota((128, 640), 1)
    unit = jnp.right_shift(n, 5)
    q = jnp.bitwise_and(jnp.right_shift(n, 1), 3)
    upper = (unit >= 10).astype(jnp.int32)
    spread = jnp.where((4 * upper + q) * 16 + unit - 10 * upper == iota((128, 640), 0), 1.0, 0.0).astype(BF16)
    n = iota((8, 640), 1)
    match = jnp.bitwise_and(jnp.right_shift(n, 3), 3) * 2 + jnp.bitwise_and(n, 1) == iota((8, 640), 0)
    keep = jnp.broadcast_to(jnp.where(match, 1.0, 0.0)[None], (32, 8, 640))

    def kron(part):
        return (jnp.broadcast_to(mm(part, spread)[:, None, :], (32, 8, 640)) * keep).reshape(256, 640)

    hi, lo = halves(Pv)
    L1h[...] = kron(hi).astype(BF16)
    L1l[...] = kron(lo).astype(BF16)
    hi, lo = halves(Pb)
    L2h[...] = jnp.transpose(kron(hi)).astype(BF16)
    L2l[...] = jnp.transpose(kron(lo)).astype(BF16)
    invT = jnp.transpose(jnp.concatenate([Zi[...], jnp.zeros((96, 128), F32)], axis=0))[:32]

    def recursion(cov, taper, out):
        gains = []
        for k in range(32):
            left_, right_ = cov[8 * k : 8 * k + 8, :128], cov[8 * k : 8 * k + 8, 128:]
            for j in range(k):
                s = jnp.broadcast_to(LB[j, k : k + 1, :], (8, 128))
                left_, right_ = left_ - s * gains[j][0], right_ - s * gains[j][1]
            t = taper(k)
            left_, right_ = left_ * t[:, 0:128], right_ * t[:, 128:256]
            gains.append((left_, right_))
            out[8 * k : 8 * k + 8, 0:128] = left_
            out[8 * k : 8 * k + 8, 128:256] = right_

    added = [corr[0], corr[1]]

    def amend_own(fl, carry):
        for m in range(10):
            y = pltpu.roll(added[m // 5], 127 - 2 * ((m % 5) * 12 + fl), 1)
            E[m, fl, :, 0:128] = F[m, fl, :, 0:128] + jnp.where(lane16 == 0, y, 0.0)
            E[m, fl, :, 128:256] = F[m, fl, :, 128:256] + jnp.where(lane16 == 127, y, 0.0)
        return carry

    lax.fori_loop(10, 12, amend_own, 0)
    own = jnp.where(iota((128, 80), 0) == me * 16 + jnp.right_shift(iota((128, 80), 1), 3), 1.0, 0.0).astype(BF16)
    keep_own = jnp.where(jnp.bitwise_and(iota((8, 80), 1), 7) == iota((8, 80), 0), 1.0, 0.0)
    keep_own = jnp.broadcast_to(keep_own[None], (32, 8, 80))

    def kron_own(part):
        return (jnp.broadcast_to(mm(part, own)[:, None, :], (32, 8, 80)) * keep_own).reshape(256, 80).astype(BF16)

    hi, lo = halves(Pv)
    own_h, own_l = kron_own(hi), kron_own(lo)
    group = jnp.right_shift(iota((256, 256), 0), 3) == jnp.right_shift(iota((256, 256), 1), 3)
    group = jnp.where(group, 1.0, 0.0).astype(BF16)
    third = jnp.where(sub8 == 2, 1.0, 0.0).astype(BF16)

    def own_sums(u, acc):
        f, h = jnp.right_shift(u, 1), jnp.bitwise_and(u, 1)
        x = E[:, 8 + f, pl.ds(pl.multiple_of(8 * h, 8), 8), :]
        xh, xl = halves(x.reshape(80, 256))
        recursion(mm(own_h, xh) + (mm(own_h, xl) + mm(own_l, xh)), lambda k: TQ[32 * h + k], Kd)
        kh, kl = halves(Kd[...])
        th, tl = halves(mm_nt(third, kh) + mm_nt(third, kl))
        here = (jnp.bitwise_and(jnp.right_shift(lane8, 1), 3) == f) & ~(jnp.bitwise_and(lane8, 1) == 1)
        return acc + jnp.where(here, mm(th, group) + mm(tl, group), 0.0)

    sums = lax.fori_loop(4, 8, own_sums, jnp.zeros((8, 256), F32))

    own_corr.wait()
    for c in fixes:
        c.wait_recv()
    first, last = iota((8, 128), 1) == 0, iota((8, 128), 1) == 127

    def amend(fl, carry):
        for u in range(20):
            y = pltpu.roll(CR[u // 10, u % 10 // 5], 127 - 2 * ((u % 5) * 12 + fl), 1)
            D[u, fl, :, 0:128] = D[u, fl, :, 0:128] + jnp.where(first, y, 0.0)
            D[u, fl, :, 128:256] = D[u, fl, :, 128:256] + jnp.where(last, y, 0.0)
        return carry

    def arrive(first_fl, end_fl):
        for u in range(first_fl, end_fl):
            locals_[u].wait()
            for c in arrivals[7 * u : 7 * u + 7]:
                c.wait_recv()
        lax.fori_loop(first_fl, end_fl, amend, 0)

    def cell_gains(g):
        arrive(4 * g if g < 2 else 10, 4 * g + 4)
        xh, xl = halves(D[:, 4 * g : 4 * g + 4].reshape(640, 256))
        cov = mm(L1h[...], xh) + (mm(L1h[...], xl) + mm(L1l[...], xh))
        recursion(cov, lambda k: TP[k], Kf.at[g])
        hi, lo = halves(Kf[g])
        Kh[g], Kl[g] = hi, lo
        pick = jnp.where(sub8 == g, 1.0, 0.0).astype(BF16)
        return mm_nt(pick, hi) + mm_nt(pick, lo)

    for g in range(2):
        sums = sums + cell_gains(g)
    arrive(8, 10)
    xh, xl = halves(jnp.concatenate([D[:, 8:10], jnp.zeros((20, 2, 8, 256), F32)], axis=1).reshape(640, 256))
    recursion(mm(L1h[...], xh) + (mm(L1h[...], xl) + mm(L1l[...], xh)), lambda k: TP[k], Kd)
    hi, lo = halves(Kd[...])
    sums = sums + (mm_nt(third, hi) + mm_nt(third, lo))
    sbuf[0] = jnp.where(sub8 == 3, wet0 + wet1, sums)
    parts = [
        remote(sbuf.at[0], sin2.at[i - 1], m2s.at[i - 1], m2r.at[i - 1], along(i)) for i in (4, 5, 2, 3, 6, 7, 1)
    ]

    outs = []

    def update(g):
        change = mm(L2h[...], Kh[g]) + (mm(L2h[...], Kl[g]) + mm(L2l[...], Kh[g]))
        D[:, 4 * g : 4 * g + 4] = D[:, 4 * g : 4 * g + 4] - change.reshape(20, 4, 8, 256)
        for s in range(8):
            c = pltpu.make_async_copy(
                D.at[pl.ds(10 * (s // 4), 10), pl.ds(4 * g, 4), pl.ds(2 * (s % 4), 2), :],
                x1_out.at[pl.ds(10 * s, 10), pl.ds(4 * g, 4), :, :],
                out_sem.at[8 * g + s],
            )
            c.start()
            outs.append(c)

    update(0)
    total = sbuf[0]
    for c in parts:
        c.wait_recv()
    for i in range(7):
        total = total + sin2[i]
    sbuf[1] = total
    parts = [
        remote(sbuf.at[1], sin1.at[i - 1], d2s.at[i - 1], d2r.at[i - 1], across(i)) for i in NEAR_LAST
    ]
    update(1)
    cell_gains(2)
    update(2)
    for c in parts:
        c.wait_recv()
    for i in range(15):
        total = total + sin1[i]

    cells = jnp.sum(jnp.sum(jnp.where(sub8 == 3, total, 0.0), axis=1, keepdims=True), axis=0, keepdims=True)
    share = total * (1.0 / jnp.broadcast_to(cells, (8, 256)))
    fl_w = jnp.concatenate([fl_s, fl_s], axis=1)
    picked = jnp.zeros((32, 256), F32)
    for g in range(3):
        picked = jnp.where(jnp.right_shift(fl_w, 2) == g, share[g : g + 1, :], picked)
    four = jnp.bitwise_and(jnp.right_shift(iota((32, 256), 1), 1), 3)
    picked = jnp.where(four == jnp.bitwise_and(fl_w, 3), picked, 0.0)
    fold = jnp.where(jnp.right_shift(iota((256, 128), 0), 3) == iota((256, 128), 1), 1.0, 0.0).astype(BF16)
    hi, lo = halves(picked)
    shifts = mm(hi, fold) + mm(lo, fold)
    shifts = jnp.where(jnp.right_shift(lane32, 3) < jnp.right_shift(sub32, 3), shifts, 0.0)
    base = val_s - ybar
    innov = jnp.sum(invT * base, axis=0, keepdims=True)
    for _ in range(3):
        moved = base + jnp.sum(shifts * innov, axis=1, keepdims=True)
        innov = jnp.sum(invT * moved, axis=0, keepdims=True)
    wide = jnp.zeros((8, 256), F32)
    mean = [jnp.zeros((8, 256), F32) for _ in range(3)]
    for k in range(32):
        dk = jnp.broadcast_to(innov[0:1, k : k + 1], (8, 256))
        wide = jnp.where(jnp.right_shift(lane8, 3) == k, dk, wide)
        mean = [mean[g] + dk * Kf[g, 8 * k : 8 * k + 8, :] for g in range(3)]
    same = jnp.bitwise_and(jnp.right_shift(lane8, 1), 3) == jnp.right_shift(sub8, 1)
    for g in range(3):
        part = jnp.where(same, share[g : g + 1, :] * wide, 0.0)
        shift = jnp.broadcast_to(jnp.sum(part, axis=1, keepdims=True), (8, 256))
        M[8 * g : 8 * g + 8, :] = mean[g] - wet8 * shift
    for fl in range(12):
        c = pltpu.make_async_copy(M.at[pl.ds(2 * fl, 2), :], mrow_out.at[fl], out_sem.at[24 + fl])
        c.start()
        outs.append(c)
    for c in outs:
        c.wait()
    for c in sends:
        c.wait_send()


def local(ensemble, velocity, diffusivity, land_mask, obs_index, obs_owner, obs_value, obs_error):
    hbm = pl.BlockSpec(memory_space=pltpu.HBM)
    vm = lambda *shape, t=F32: pltpu.VMEM(shape, t)
    dma = lambda n: pltpu.SemaphoreType.DMA((n,))
    x1, mrow = pl.pallas_call(
        kernel,
        out_shape=(jax.ShapeDtypeStruct((80, 12, 2, 256), F32), jax.ShapeDtypeStruct((12, 2, 256), F32)),
        in_specs=[hbm] * 8,
        out_specs=(pl.BlockSpec(memory_space=pl.ANY), pl.BlockSpec(memory_space=pl.ANY)),
        scratch_shapes=[
            pltpu.SMEM((4,), F32), pltpu.SMEM((4, 4, 8), jnp.int32), pltpu.SMEM((4,), jnp.int32),
            pltpu.SMEM((4, 8), F32), pltpu.SMEM((4, 8), F32),
            vm(10, 12, 16, 256), vm(2, 3, 16, 256), vm(16, 256, t=jnp.int32), vm(10, 12, 16, 256),
            vm(20, 12, 8, 256), vm(2, 16, 128), vm(2, 2, 16, 128), vm(2, 16, 128), vm(2, 2, 8, 128),
            vm(8, 128), vm(16, 128), vm(16, 8, 128), vm(7, 8, 8, 128), vm(8, 8, 128), vm(32, 32, 128), vm(32, 8, 256),
            vm(32, 128), vm(32, 128), vm(32, 128), vm(32, 128), vm(32, 32, 128),
            vm(256, 640, t=BF16), vm(256, 640, t=BF16), vm(640, 256, t=BF16), vm(640, 256, t=BF16),
            vm(3, 256, 256), vm(3, 256, 256, t=BF16), vm(3, 256, 256, t=BF16),
            vm(2, 8, 256), vm(15, 8, 256), vm(7, 8, 256), vm(24, 256), vm(64, 8, 256), vm(256, 256),
            dma(10), dma(13), dma(36), dma(2), dma(2), dma(7), dma(7), dma(84), dma(84),
            dma(15), dma(15), dma(7), dma(7), dma(15), dma(15), dma(7), dma(7),
        ],
        compiler_params=pltpu.CompilerParams(collective_id=0, has_side_effects=True, vmem_limit_bytes=58 << 20),
    )(
        ensemble.reshape(10, 12, 16, 256),
        velocity,
        land_mask,
        diffusivity,
        jnp.transpose(obs_index, (0, 2, 1)),
        obs_owner,
        obs_value,
        obs_error,
    )
    return (x1 + mrow[None]).reshape(80, 4, 3, 2, 256)


def solution(mesh):
    in_specs = (
        P("member", None, None, None, "domain"),
        P(None, None, None, "domain"),
        P(),
        P(None, "domain"),
        P(),
        P(),
        P(),
        P(),
    )
    out_specs = P(None, None, None, "member", "domain")
    return jax.shard_map(local, mesh=mesh, in_specs=in_specs, out_specs=out_specs, check_vma=False)
```

```python
import jax
import jax.numpy as jnp
from jax import lax
from jax.experimental import pallas as pl
from jax.experimental.pallas import tpu as pltpu
from jax.sharding import PartitionSpec as P

LOC_RADIUS = 64.0
MEM, DOM = 8, 16
FAR_FIRST = (5, 3, 7, 4, 1, 2, 6)
NEAR_LAST = (5, 13, 3, 7, 11, 15, 12, 4, 1, 9, 10, 14, 2, 6, 8)
MESH = pl.DeviceIdType.MESH
F32, BF16 = jnp.float32, jnp.bfloat16
HIGH = lax.Precision.HIGHEST


def gaspari(distance):
    scaled = distance * (1.0 / LOC_RADIUS)
    safe = jnp.maximum(scaled, 1.0)
    near = (((-0.25 * scaled + 0.5) * scaled + 0.625) * scaled - 5.0 / 3.0) * scaled * scaled + 1.0
    far = (
        ((((scaled * (1.0 / 12.0) - 0.5) * scaled + 0.625) * scaled + 5.0 / 3.0) * scaled - 5.0) * scaled
        + 4.0
        - (2.0 / 3.0) / safe
    )
    return jnp.where(scaled <= 1.0, near, jnp.where(scaled < 2.0, far, 0.0))


def separation(row_a, col_a, row_b, col_b):
    gap = jnp.abs(col_a - col_b)
    gap = jnp.minimum(gap, 4096 - gap)
    rows = row_a - row_b
    return jnp.sqrt((gap * gap + rows * rows).astype(F32))


def iota(shape, dim):
    return lax.broadcasted_iota(jnp.int32, shape, dim)


def halves(x):
    hi = x.astype(BF16)
    return hi, (x - hi.astype(F32)).astype(BF16)


def mm(a, b):
    return jnp.dot(a, b, preferred_element_type=F32)


def mm_nt(a, b, precision=None):
    return lax.dot_general(a, b, (((1,), (1,)), ((), ())), precision=precision, preferred_element_type=F32)


def kernel(
    ens, vel, mask, diff_in, oidx_in, oown_in, oval_in, oerr_in, x1_out, mrow_out,
    diff, oidx, oown, oval, oerr, E, V, W, F, D, pack, halo, corr, CR, vbuf, vtmp, vin, vin2, Z, RB, TP, Pm, Zi, bcol, gcol, LB,
    L1h, L1l, L2h, L2l, Kf, Kh, Kl, sbuf, sin1, sin2, M,
    in_sem, loc_sem, out_sem, hs, hr, cs, cr, as_, ar, d1s, d1r, m1s, m1r, d2s, d2r, m2s, m2r,
):
    me, dom = lax.axis_index("member"), lax.axis_index("domain")

    small = ((vel, V), (mask, W), (diff_in, diff), (oidx_in, oidx), (oown_in, oown), (oval_in, oval), (oerr_in, oerr))
    small = [pltpu.make_async_copy(src, dst, in_sem.at[3 + i]) for i, (src, dst) in enumerate(small)]
    copies = []
    for g in range(3):
        copies.append(pltpu.make_async_copy(ens.at[:, pl.ds(4 * g, 4)], E.at[:, pl.ds(4 * g, 4)], in_sem.at[g]))
    for c in small + copies:
        c.start()
    barrier = pltpu.get_barrier_semaphore()
    right, left = lax.rem(dom + 1, DOM), lax.rem(dom + DOM - 1, DOM)

    def across(i):
        return {"member": jnp.bitwise_xor(me, i % 8), "domain": jnp.bitwise_xor(dom, 8 * (i // 8))}

    def along(i):
        return {"domain": jnp.bitwise_xor(dom, i)}

    for where in [across(i) for i in range(1, 16)] + [along(i) for i in range(1, 8)]:
        pl.semaphore_signal(barrier, inc=1, device_id=where, device_id_type=MESH)
    for where in (left, right):
        pl.semaphore_signal(barrier, inc=1, device_id={"domain": where}, device_id_type=MESH)
    for c in small:
        c.wait()

    wet = W[...].astype(F32)
    row, col = iota((16, 256), 0), iota((16, 256), 1)
    lane16 = iota((16, 128), 1)
    even = jnp.bitwise_and(lane16, 1) == 0
    slot_fl = jnp.right_shift(lane16, 1)
    for _ in range(4):
        slot_fl = jnp.where(slot_fl >= 12, slot_fl - 12, slot_fl)
    slot_fl = jnp.where(lane16 < 120, slot_fl, -1)

    def interior(fl, acc):
        acc = list(acc)
        lev, fld = lax.rem(fl, 3), lax.div(fl, 3)
        u, v, d = V[0, lev], V[1, lev], diff[fld]
        cen = wet * (1.0 - 4.0 * d)
        east, west = wet * (d - 0.5 * u), wet * (d + 0.5 * u)
        north, south = wet * (d - 0.5 * v), wet * (d + 0.5 * v)
        ours = slot_fl == fl
        acc[2] = jnp.where(ours & even, jnp.broadcast_to(east[:, 255:256], (16, 128)), acc[2])
        acc[2] = jnp.where(ours & ~even, jnp.broadcast_to(west[:, 0:1], (16, 128)), acc[2])
        east, west = jnp.where(col == 255, 0.0, east), jnp.where(col == 0, 0.0, west)
        north, south = jnp.where(row == 15, 0.0, north), jnp.where(row == 0, 0.0, south)
        for m in range(10):
            x = E[m, fl]
            F[m, fl] = (
                cen * x
                + east * pltpu.roll(x, 255, 1)
                + west * pltpu.roll(x, 1, 1)
                + north * pltpu.roll(x, 15, 0)
                + south * pltpu.roll(x, 1, 0)
            )
            slot = 2 * ((m % 5) * 12 + fl)
            edges = pltpu.roll(jnp.where(lane16 == 0, x[:, :128], x[:, 128:]), slot, 1)
            here = (lane16 == slot) | (lane16 == jnp.bitwise_and(slot + 127, 127))
            acc[m // 5] = jnp.where(here, edges, acc[m // 5])
        return tuple(acc)

    acc = tuple(jnp.zeros((16, 128), F32) for _ in range(3))
    copies[0].wait()
    acc = lax.fori_loop(0, 4, interior, acc)

    pl.semaphore_wait(barrier, 24)
    sends = []

    def remote(src, dst, send, recv, where):
        c = pltpu.make_async_remote_copy(
            src_ref=src, dst_ref=dst, send_sem=send, recv_sem=recv, device_id=where, device_id_type=MESH
        )
        c.start()
        sends.append(c)
        return c

    arrivals, locals_ = [], []
    own_rows, own_slot = pl.ds(2 * me, 2), pl.ds(2 * lax.rem(me, 4), 2)
    half = lax.div(me, 4)

    def scatter(g):
        fls = pl.ds(g, 1)
        mine = D.at[pl.ds(10 * half, 10), fls, own_slot, :]
        c = pltpu.make_async_copy(F.at[:, fls, own_rows, :], mine, loc_sem.at[g])
        c.start()
        locals_.append(c)
        for i in FAR_FIRST:
            t = jnp.bitwise_xor(me, i)
            n = 7 * g + i - 1
            arrivals.append(remote(F.at[:, fls, pl.ds(2 * t, 2), :], mine, as_.at[n], ar.at[n], {"member": t}))

    scatter(0)
    scatter(1)
    for g in (1, 2):
        copies[g].wait()
        acc = lax.fori_loop(4 * g, 4 * g + 4, interior, acc)
    pack[0], pack[1] = acc[0], acc[1]

    to_left = remote(pack, halo.at[0], hs.at[0], hr.at[0], {"domain": left})
    to_right = remote(pack, halo.at[1], hs.at[1], hr.at[1], {"domain": right})

    lane32, sub32 = iota((32, 128), 1), iota((32, 128), 0)

    def wide_l(x, rows):
        return jnp.broadcast_to(x[0:1, :], (rows, 128))

    zi = jnp.zeros((32, 128), jnp.int32)
    row_s, col_s, fl_s, row_l, col_l, fl_l = zi, zi, zi, zi, zi, zi
    val_s = jnp.zeros((32, 128), F32)
    places = []
    for k in range(32):
        b, n = k // 8, k % 8
        own = oown[b]
        r = jnp.right_shift(own, 4) * 2 + oidx[b, 2, n]
        c = jnp.bitwise_and(own, 15) * 256 + oidx[b, 3, n]
        f = oidx[b, 0, n] * 3 + oidx[b, 1, n]
        places.append((r, c))
        row_s, col_s, fl_s = (jnp.where(sub32 == k, s, a) for s, a in ((r, row_s), (c, col_s), (f, fl_s)))
        row_l, col_l, fl_l = (jnp.where(lane32 == k, s, a) for s, a in ((r, row_l), (c, col_l), (f, fl_l)))
        val_s = jnp.where(sub32 == k, oval[b, n], val_s)
    pick = (iota((256, 128), 0) + dom * 256 == wide_l(col_l, 256)) & (iota((256, 128), 1) < 32)
    pick = jnp.where(pick, 1.0, 0.0).astype(BF16)
    at_row = jnp.bitwise_and(iota((160, 128), 0), 15) == wide_l(row_l, 160)
    got = jnp.zeros((160, 128), F32)
    for fl in range(12):
        x = F[:, fl].reshape(160, 256)
        hi = x.astype(BF16)
        rest = x - hi.astype(F32)
        mid, lo = halves(rest)
        got = jnp.where(wide_l(fl_l, 160) == fl, mm(hi, pick) + (mm(mid, pick) + mm(lo, pick)), got)
    got = jnp.where(at_row, got, 0.0)
    seen = jnp.sum(got.reshape(10, 16, 128), axis=1)
    tile_l, edge_l = jnp.right_shift(col_l, 8), jnp.bitwise_and(col_l, 255)
    some = lane32 < 32
    at_last, at_first = some & (edge_l == 255), some & (edge_l == 0)
    spot = jnp.where(at_first & (jnp.bitwise_and(tile_l + 15, 15) == dom), 2 * fl_l - 1, -1000)
    spot = jnp.where(at_last & (jnp.bitwise_and(tile_l + 1, 15) == dom), 2 * fl_l, spot)
    coef = jnp.where(at_first & (tile_l == dom), 2 * fl_l + 1, jnp.where(at_last & (tile_l == dom), 2 * fl_l, -1000))
    spot, coef = wide_l(pltpu.roll(spot, 32, 1), 128), wide_l(pltpu.roll(coef, 64, 1), 128)
    picks = [spot + 24 * u for u in range(5)]
    picks = [jnp.where(p == -1, 127, p) for p in picks] + [coef]
    picks = jnp.concatenate([jnp.where(iota((128, 128), 0) == p, 1.0, 0.0).astype(BF16) for p in picks], axis=1)
    rest = jnp.concatenate([acc[0], acc[1], acc[2]], axis=0)
    hi = rest.astype(BF16)
    mid, lo = halves(rest - hi.astype(F32))
    extra = mm(hi, picks) + (mm(mid, picks) + mm(lo, picks))
    in_row = iota((16, 128), 0) == wide_l(pltpu.roll(row_l, 32, 1), 16)
    in_row2 = iota((16, 128), 0) == wide_l(pltpu.roll(row_l, 64, 1), 16)
    vtmp[...] = jnp.zeros((16, 128), F32)
    for m in range(10):
        part = extra[16 * (m // 5) : 16 * (m // 5) + 16, 128 * (m % 5) : 128 * (m % 5) + 128]
        vtmp[m : m + 1, :] = seen[m : m + 1, :] + jnp.sum(jnp.where(in_row, part, 0.0), axis=0, keepdims=True)
    part = jnp.sum(jnp.where(in_row2, extra[32:48, 640:768], 0.0), axis=0, keepdims=True)
    high = pltpu.roll(vtmp[8:16, :], 64, 1)
    vbuf[...] = vtmp[0:8, :] + jnp.where(iota((8, 128), 0) == 2, part, high)
    parts_a = [
        remote(vbuf, vin.at[i], d1s.at[i - 1], d1r.at[i - 1], across(i)) for i in NEAR_LAST
    ]
    for g in range(2, 5):
        scatter(g)

    to_left.wait_recv()
    to_right.wait_recv()
    for h in range(2):
        corr[h] = jnp.where(even, halo[0, h], pltpu.roll(halo[1, h], 2, 1)) * acc[2]
    fixes = []
    mine = CR.at[half, :, own_slot, :]
    own_corr = pltpu.make_async_copy(corr.at[:, own_rows, :], mine, loc_sem.at[12])
    own_corr.start()
    for i in FAR_FIRST:
        t = jnp.bitwise_xor(me, i)
        fixes.append(remote(corr.at[:, pl.ds(2 * t, 2), :], mine, cs.at[i - 1], cr.at[i - 1], {"member": t}))
    for g in range(5, 12):
        scatter(g)

    rho = gaspari(separation(row_s, col_s, row_l, col_l))
    for k in range(32):
        RB[k] = jnp.broadcast_to(rho[:, k : k + 1], (32, 128))


    sub8, lane8 = iota((8, 256), 0), iota((8, 256), 1)
    odd = jnp.bitwise_and(sub8, 1) == 1
    wet0 = jnp.broadcast_to(W[pl.ds(2 * me, 1), :].astype(F32), (8, 256))
    wet1 = jnp.broadcast_to(W[pl.ds(2 * me + 1, 1), :].astype(F32), (8, 256))
    wet8 = jnp.where(odd, wet1, wet0)
    row8, col8 = 2 * me + jnp.bitwise_and(sub8, 1), dom * 256 + lane8
    for k in range(32):
        TP[k] = gaspari(separation(row8, col8, places[k][0], places[k][1])) * wet8

    for c in parts_a:
        c.wait_recv()
    vin[0] = vbuf[...]
    for i in range(8):
        Z[jnp.bitwise_xor(me, i)] = vin[i] + vin[i + 8]
    parts_b = [remote(Z, vin2.at[i - 1], m1s.at[i - 1], m1r.at[i - 1], along(i)) for i in (4, 5, 2, 3, 6, 7, 1)]
    for c in parts_b:
        c.wait_recv()
    total = Z[...]
    for i in range(7):
        total = total + vin2[i]
    total = jnp.concatenate([total, pltpu.roll(total, 64, 2)], axis=1)

    Y = jnp.transpose(total.reshape(128, 128))
    real = jnp.bitwise_and(lane32, 15) < 10
    Y = jnp.where(real, Y[0:32] + Y[32:64] * jnp.broadcast_to(Y[0:32, 10:11], (32, 128)), 0.0)
    ybar = jnp.broadcast_to(jnp.sum(Y, axis=1, keepdims=True) * (1.0 / 80.0), (32, 128))
    A = jnp.where(real, Y - ybar, 0.0)
    inv = jnp.where(lane32 == sub32, 1.0, 0.0).astype(F32)
    for k in range(32):
        a, z = A[k : k + 1, :], inv[k : k + 1, :]
        cov = jnp.broadcast_to(jnp.sum(A * a, axis=1, keepdims=True), (32, 128))
        err = oerr[k // 8, k % 8]
        den = cov[k : k + 1, :] * (1.0 / 79.0) + err
        gain = 1.0 / (79.0 * den)
        beta = 1.0 / (1.0 + jnp.sqrt(err / den))
        Pm[k : k + 1, :] = a
        Zi[k : k + 1, :] = z
        bcol[k : k + 1, :] = beta
        gcol[k : k + 1, :] = gain
        step = RB[k] * cov * gain
        A = A - (step * beta) * a
        inv = inv - step * z

    Pv = Pm[...]
    Pb = Pv * bcol[...]
    low = mm_nt(Pv, Pb, HIGH)
    for j in range(31):
        LB[j] = jnp.broadcast_to(low[:, j : j + 1], (32, 128))
    for k in range(32):
        TP[k] = TP[k] * jnp.broadcast_to(gcol[k : k + 1, 0:1], (8, 256))

    n = iota((128, 640), 1)
    unit = jnp.right_shift(n, 5)
    q = jnp.bitwise_and(jnp.right_shift(n, 1), 3)
    upper = (unit >= 10).astype(jnp.int32)
    spread = jnp.where((4 * upper + q) * 16 + unit - 10 * upper == iota((128, 640), 0), 1.0, 0.0).astype(BF16)
    n = iota((8, 640), 1)
    match = jnp.bitwise_and(jnp.right_shift(n, 3), 3) * 2 + jnp.bitwise_and(n, 1) == iota((8, 640), 0)
    keep = jnp.broadcast_to(jnp.where(match, 1.0, 0.0)[None], (32, 8, 640))

    def kron(part):
        return (jnp.broadcast_to(mm(part, spread)[:, None, :], (32, 8, 640)) * keep).reshape(256, 640)

    hi, lo = halves(Pv)
    L1h[...] = kron(hi).astype(BF16)
    L1l[...] = kron(lo).astype(BF16)
    hi, lo = halves(Pb)
    L2h[...] = jnp.transpose(kron(hi)).astype(BF16)
    L2l[...] = jnp.transpose(kron(lo)).astype(BF16)
    invT = jnp.transpose(jnp.concatenate([Zi[...], jnp.zeros((96, 128), F32)], axis=0))[:32]

    sums = jnp.zeros((8, 256), F32)
    own_corr.wait()
    for c in fixes:
        c.wait_recv()
    first, last = iota((8, 128), 1) == 0, iota((8, 128), 1) == 127

    def amend(fl, carry):
        for u in range(20):
            y = pltpu.roll(CR[u // 10, u % 10 // 5], 127 - 2 * ((u % 5) * 12 + fl), 1)
            D[u, fl, :, 0:128] = D[u, fl, :, 0:128] + jnp.where(first, y, 0.0)
            D[u, fl, :, 128:256] = D[u, fl, :, 128:256] + jnp.where(last, y, 0.0)
        return carry

    for g in range(3):
        for u in range(4 * g, 4 * g + 4):
            locals_[u].wait()
            for c in arrivals[7 * u : 7 * u + 7]:
                c.wait_recv()
        lax.fori_loop(4 * g, 4 * g + 4, amend, 0)
        xh, xl = halves(D[:, 4 * g : 4 * g + 4].reshape(640, 256))
        cov = mm(L1h[...], xh) + (mm(L1h[...], xl) + mm(L1l[...], xh))
        gains = []
        for k in range(32):
            left_, right_ = cov[8 * k : 8 * k + 8, :128], cov[8 * k : 8 * k + 8, 128:]
            for j in range(k):
                s = jnp.broadcast_to(LB[j, k : k + 1, :], (8, 128))
                left_, right_ = left_ - s * gains[j][0], right_ - s * gains[j][1]
            left_, right_ = left_ * TP[k, :, 0:128], right_ * TP[k, :, 128:256]
            gains.append((left_, right_))
            Kf[g, 8 * k : 8 * k + 8, 0:128] = left_
            Kf[g, 8 * k : 8 * k + 8, 128:256] = right_
        hi, lo = halves(Kf[g])
        Kh[g], Kl[g] = hi, lo
        pick = jnp.where(sub8 == g, 1.0, 0.0).astype(BF16)
        sums = sums + (mm_nt(pick, hi) + mm_nt(pick, lo))
    sbuf[0] = jnp.where(sub8 == 3, wet0 + wet1, sums)
    parts = [
        remote(sbuf.at[0], sin2.at[i - 1], m2s.at[i - 1], m2r.at[i - 1], along(i)) for i in (4, 5, 2, 3, 6, 7, 1)
    ]

    outs = []

    def update(g):
        change = mm(L2h[...], Kh[g]) + (mm(L2h[...], Kl[g]) + mm(L2l[...], Kh[g]))
        D[:, 4 * g : 4 * g + 4] = D[:, 4 * g : 4 * g + 4] - change.reshape(20, 4, 8, 256)
        for s in range(8):
            c = pltpu.make_async_copy(
                D.at[pl.ds(10 * (s // 4), 10), pl.ds(4 * g, 4), pl.ds(2 * (s % 4), 2), :],
                x1_out.at[pl.ds(10 * s, 10), pl.ds(4 * g, 4), :, :],
                out_sem.at[8 * g + s],
            )
            c.start()
            outs.append(c)

    update(0)
    update(1)
    total = sbuf[0]
    for c in parts:
        c.wait_recv()
    for i in range(7):
        total = total + sin2[i]
    sbuf[1] = total
    parts = [
        remote(sbuf.at[1], sin1.at[i - 1], d2s.at[i - 1], d2r.at[i - 1], across(i)) for i in NEAR_LAST
    ]
    update(2)
    for c in parts:
        c.wait_recv()
    for i in range(15):
        total = total + sin1[i]

    cells = jnp.sum(jnp.sum(jnp.where(sub8 == 3, total, 0.0), axis=1, keepdims=True), axis=0, keepdims=True)
    share = total * (1.0 / jnp.broadcast_to(cells, (8, 256)))
    fl_w = jnp.concatenate([fl_s, fl_s], axis=1)
    picked = jnp.zeros((32, 256), F32)
    for g in range(3):
        picked = jnp.where(jnp.right_shift(fl_w, 2) == g, share[g : g + 1, :], picked)
    four = jnp.bitwise_and(jnp.right_shift(iota((32, 256), 1), 1), 3)
    picked = jnp.where(four == jnp.bitwise_and(fl_w, 3), picked, 0.0)
    fold = jnp.where(jnp.right_shift(iota((256, 128), 0), 3) == iota((256, 128), 1), 1.0, 0.0).astype(BF16)
    hi, lo = halves(picked)
    shifts = mm(hi, fold) + mm(lo, fold)
    shifts = jnp.where(jnp.right_shift(lane32, 3) < jnp.right_shift(sub32, 3), shifts, 0.0)
    base = val_s - ybar
    innov = jnp.sum(invT * base, axis=0, keepdims=True)
    for _ in range(3):
        moved = base + jnp.sum(shifts * innov, axis=1, keepdims=True)
        innov = jnp.sum(invT * moved, axis=0, keepdims=True)
    wide = jnp.zeros((8, 256), F32)
    mean = [jnp.zeros((8, 256), F32) for _ in range(3)]
    for k in range(32):
        dk = jnp.broadcast_to(innov[0:1, k : k + 1], (8, 256))
        wide = jnp.where(jnp.right_shift(lane8, 3) == k, dk, wide)
        mean = [mean[g] + dk * Kf[g, 8 * k : 8 * k + 8, :] for g in range(3)]
    same = jnp.bitwise_and(jnp.right_shift(lane8, 1), 3) == jnp.right_shift(sub8, 1)
    for g in range(3):
        part = jnp.where(same, share[g : g + 1, :] * wide, 0.0)
        shift = jnp.broadcast_to(jnp.sum(part, axis=1, keepdims=True), (8, 256))
        M[8 * g : 8 * g + 8, :] = mean[g] - wet8 * shift
    for fl in range(12):
        c = pltpu.make_async_copy(M.at[pl.ds(2 * fl, 2), :], mrow_out.at[fl], out_sem.at[24 + fl])
        c.start()
        outs.append(c)
    for c in outs:
        c.wait()
    for c in sends:
        c.wait_send()


def local(ensemble, velocity, diffusivity, land_mask, obs_index, obs_owner, obs_value, obs_error):
    hbm = pl.BlockSpec(memory_space=pltpu.HBM)
    vm = lambda *shape, t=F32: pltpu.VMEM(shape, t)
    dma = lambda n: pltpu.SemaphoreType.DMA((n,))
    x1, mrow = pl.pallas_call(
        kernel,
        out_shape=(jax.ShapeDtypeStruct((80, 12, 2, 256), F32), jax.ShapeDtypeStruct((12, 2, 256), F32)),
        in_specs=[hbm] * 8,
        out_specs=(pl.BlockSpec(memory_space=pl.ANY), pl.BlockSpec(memory_space=pl.ANY)),
        scratch_shapes=[
            pltpu.SMEM((4,), F32), pltpu.SMEM((4, 4, 8), jnp.int32), pltpu.SMEM((4,), jnp.int32),
            pltpu.SMEM((4, 8), F32), pltpu.SMEM((4, 8), F32),
            vm(10, 12, 16, 256), vm(2, 3, 16, 256), vm(16, 256, t=jnp.int32), vm(10, 12, 16, 256),
            vm(20, 12, 8, 256), vm(2, 16, 128), vm(2, 2, 16, 128), vm(2, 16, 128), vm(2, 2, 8, 128),
            vm(8, 128), vm(16, 128), vm(16, 8, 128), vm(7, 8, 8, 128), vm(8, 8, 128), vm(32, 32, 128), vm(32, 8, 256),
            vm(32, 128), vm(32, 128), vm(32, 128), vm(32, 128), vm(32, 32, 128),
            vm(256, 640, t=BF16), vm(256, 640, t=BF16), vm(640, 256, t=BF16), vm(640, 256, t=BF16),
            vm(3, 256, 256), vm(3, 256, 256, t=BF16), vm(3, 256, 256, t=BF16),
            vm(2, 8, 256), vm(15, 8, 256), vm(7, 8, 256), vm(24, 256),
            dma(10), dma(13), dma(36), dma(2), dma(2), dma(7), dma(7), dma(84), dma(84),
            dma(15), dma(15), dma(7), dma(7), dma(15), dma(15), dma(7), dma(7),
        ],
        compiler_params=pltpu.CompilerParams(collective_id=0, has_side_effects=True, vmem_limit_bytes=58 << 20),
    )(
        ensemble.reshape(10, 12, 16, 256),
        velocity,
        land_mask,
        diffusivity,
        jnp.transpose(obs_index, (0, 2, 1)),
        obs_owner,
        obs_value,
        obs_error,
    )
    return (x1 + mrow[None]).reshape(80, 4, 3, 2, 256)


def solution(mesh):
    in_specs = (
        P("member", None, None, None, "domain"),
        P(None, None, None, "domain"),
        P(),
        P(None, "domain"),
        P(),
        P(),
        P(),
        P(),
    )
    out_specs = P(None, None, None, "member", "domain")
    return jax.shard_map(local, mesh=mesh, in_specs=in_specs, out_specs=out_specs, check_vma=False)
```
